512 devices in a mesh: gx: 16 (over x_hi, y, core), gy: 32 (over z, x_lo).
Axes of the slice: x: 4 (x_hi: 2, x_lo: 2; x = x_hi * 2 + x_lo), y: 4, z: 16, core: 2. Of those that a mesh axis runs over, the one named last changes fastest.
Arguments:
- phase: float32 [128, 256, 256], P('gx', 'gy'), may hold values from -1 to 1
- solute: float32 [128, 256, 256], P('gx', 'gy'), may hold values from -0.5 to 0.5
- grain: int32 [128, 256, 256], P('gx', 'gy'), may hold values from 0 to 15
- grain_angle: float32 [16], replicated, may hold values from -3.140625 to 3.140625
- inlet_flags: int32 [256, 256], P('gy', 'gx'), may hold values 0 or 1
- populations: float32 [19, 256, 256, 128], P(None, 'gy', 'gx'), may hold values from 0.4 to 1.6
Outputs:
- phase_next: float32 [128, 256, 256], P('gx', 'gy')
- solute_next: float32 [128, 256, 256], P('gx', 'gy')
- populations_next: float32 [19, 256, 256, 128], P(None, 'gy', 'gx')
The draws below stay inside these ranges and needn't reach their ends.
All inputs are finite; a program needn't handle non-finite values. No bound on the sum of `inlet_flags` on one device may be relied on, other than what follows from the above.
Results may differ from the reference program's by a relative error of at most 0.00002.
Values sent between devices are 32-bit elements; how exact they have to be, the bound alone decides.
A program may use at most 64 MiB of HBM per device.

```python
import jax
import jax.numpy as jnp

GRAINS = 16
LB_STEPS = 2
NX = 128
NY = 256
NZ = 256


def set_ends(drawn, key, low, top_value):
    longest = drawn.shape.index(max(drawn.shape))
    spots = []
    for shift in (0, 1):
        where = [jax.random.randint(jax.random.fold_in(key, axis), (), 0, length) for axis, length in enumerate(drawn.shape)]
        where[longest] = (where[longest] + shift) % drawn.shape[longest]
        spots.append(tuple(where))
    return drawn.at[spots[0]].set(low).at[spots[1]].set(top_value)


def shard_levels(stream_key, dims, pieces, low, high):
    def one(dim, parts):
        draws = jax.random.uniform(jax.random.fold_in(jax.random.fold_in(stream_key, 6), dim), (parts,), jnp.float32, low / len(pieces), high / len(pieces))
        return jnp.repeat(jnp.exp(draws), dims[dim] // parts).reshape((-1,) + (1,) * (len(dims) - dim - 1))

    level = one(*pieces[0])
    for cut in pieces[1:]:
        level = level * one(*cut)
    return level


def setup_inputs(seed: int = 0) -> dict:
    arg_keys = jax.random.split(jax.random.key(seed), 7)
    phase = jnp.clip(jax.random.uniform(arg_keys[0], (NX, NY, NZ), jnp.float32, -1.0, 1.0) * shard_levels(arg_keys[0], (NX, NY, NZ), ((0, 16), (1, 32)), -0.4, 0.0), -1.0, 1.0)
    solute = jnp.clip(jax.random.uniform(arg_keys[1], (NX, NY, NZ), jnp.float32, -0.5, 0.5) * shard_levels(arg_keys[1], (NX, NY, NZ), ((0, 16), (1, 32)), -0.4, 0.0), -0.5, 0.5)
    grain = set_ends(jax.random.randint(arg_keys[2], (NX, NY, NZ), 0, GRAINS), jax.random.fold_in(arg_keys[2], 1), 0, GRAINS - 1).astype(jnp.int32)
    grain_angle = jnp.clip(jax.random.uniform(arg_keys[3], (GRAINS,), jnp.float32, -3.140625, 3.140625), -3.140625, 3.140625)
    inlet_flags = set_ends((jax.random.randint(arg_keys[4], (NY, NZ), 0, 4) < 3).astype(jnp.int32), jax.random.fold_in(arg_keys[4], 1), 0, 1)
    populations = jnp.clip(0.4 + 1.2 * jax.random.uniform(arg_keys[5], (19, NY, NZ, NX), jnp.float32) ** shard_levels(arg_keys[5], (19, NY, NZ, NX), ((1, 32), (2, 16)), -0.2, 0.2), 0.4, 1.6)
    return dict(phase=phase, solute=solute, grain=grain, grain_angle=grain_angle, inlet_flags=inlet_flags, populations=populations)


VELOCITY = ((0, 0, 0), (1, 0, 0), (-1, 0, 0), (0, 1, 0), (0, -1, 0), (0, 0, 1), (0, 0, -1),
            (1, 1, 0), (-1, -1, 0), (1, -1, 0), (-1, 1, 0), (1, 0, 1), (-1, 0, -1), (1, 0, -1),
            (-1, 0, 1), (0, 1, 1), (0, -1, -1), (0, 1, -1), (0, -1, 1))
WEIGHTS = (1.0 / 3.0,) + (1.0 / 18.0,) * 6 + (1.0 / 36.0,) * 12
OPPOSITE = (0, 2, 1, 4, 3, 6, 5, 8, 7, 10, 9, 12, 11, 14, 13, 16, 15, 18, 17)
TIME_STEP = 0.08
DIFFUSION = 2.0
COUPLING = 1.5
ANISO_STRENGTH = 0.3
RELAX_TIME = 0.8
BODY_FORCE = 0.01


def collide(fields, solid):
    density = fields[0]
    mom_x = jnp.zeros_like(solid)
    mom_y = jnp.zeros_like(solid)
    mom_z = jnp.zeros_like(solid)
    for comp in range(1, 19):
        density = density + fields[comp]
    for comp in range(19):
        vel = VELOCITY[comp]
        mom_x = mom_x + vel[0] * fields[comp]
        mom_y = mom_y + vel[1] * fields[comp]
        mom_z = mom_z + vel[2] * fields[comp]
    vel_x = (mom_x + 0.5 * BODY_FORCE) / density
    vel_y = mom_y / density
    vel_z = mom_z / density
    speed_sq = vel_x * vel_x + vel_y * vel_y + vel_z * vel_z
    posts = []
    for comp in range(19):
        vel = VELOCITY[comp]
        along = vel[0] * vel_x + vel[1] * vel_y + vel[2] * vel_z
        equil = WEIGHTS[comp] * density * (1.0 + 3.0 * along + 4.5 * along * along - 1.5 * speed_sq)
        relaxed = fields[comp] - (fields[comp] - equil) / RELAX_TIME + 3.0 * WEIGHTS[comp] * vel[0] * BODY_FORCE
        posts.append((1.0 - solid) * relaxed + solid * fields[OPPOSITE[comp]])
    return posts


def phase_update(phase, solute, xplus, xminus, yplus, yminus, zplus, zminus, cos_cell, sin_cell):
    laplace_phase = (xplus[0] + xminus[0]) + (yplus[0] + yminus[0]) + (zplus[0] + zminus[0]) - 6.0 * phase
    laplace_solute = (xplus[1] + xminus[1]) + (yplus[1] + yminus[1]) + (zplus[1] + zminus[1]) - 6.0 * solute
    grad_x = 0.5 * (xplus[0] - xminus[0])
    grad_y = 0.5 * (yplus[0] - yminus[0])
    square_x = grad_x * grad_x
    square_y = grad_y * grad_y
    denom = square_x + square_y + 0.25
    denom = denom * denom
    cos_four = (square_x * square_x - 6.0 * square_x * square_y + square_y * square_y) / denom
    sin_four = 4.0 * grad_x * grad_y * (square_x - square_y) / denom
    aniso = 1.0 + ANISO_STRENGTH * (cos_four * cos_cell + sin_four * sin_cell)
    bulk = 1.0 - phase * phase
    phase_next = phase + TIME_STEP * aniso * aniso * (laplace_phase + phase - phase * phase * phase - COUPLING * solute * bulk * bulk)
    solute_next = solute + TIME_STEP * DIFFUSION * laplace_solute + 0.5 * (phase_next - phase)
    return phase_next, solute_next


def reference(phase, solute, grain, grain_angle, inlet_flags, populations):
    stacked = jnp.stack([phase, solute])
    xplus = jnp.roll(stacked, -1, 1)
    xminus = jnp.roll(stacked, 1, 1)
    yplus = jnp.roll(stacked, -1, 2)
    yminus = jnp.roll(stacked, 1, 2)
    zplus = jnp.roll(stacked, -1, 3)
    zminus = jnp.roll(stacked, 1, 3)
    cos_cell = jnp.cos(4.0 * grain_angle)[grain]
    sin_cell = jnp.sin(4.0 * grain_angle)[grain]
    phase_next, solute_next = phase_update(phase, solute, xplus, xminus, yplus, yminus, zplus, zminus, cos_cell, sin_cell)
    solid = jnp.clip(0.5 * (1.0 + phase_next), 0.0, 1.0)
    solid_p = jnp.transpose(solid, (1, 2, 0))
    solid_p = solid_p.at[:, :, 0].set(jnp.where(inlet_flags == 0, 1.0, solid_p[:, :, 0]))
    fields = [populations[comp] * WEIGHTS[comp] for comp in range(19)]
    for step in range(LB_STEPS):
        posts = collide(fields, solid_p)
        fields = [jnp.roll(posts[comp], (VELOCITY[comp][1], VELOCITY[comp][2], VELOCITY[comp][0]), (0, 1, 2)) for comp in range(19)]
    populations_next = jnp.stack([fields[comp] / WEIGHTS[comp] for comp in range(19)])
    return phase_next, solute_next, populations_next
```

```python
import functools

import jax
import jax.numpy as jnp
from jax import lax
from jax.experimental import pallas as pl
from jax.experimental.pallas import tpu as pltpu
from jax.sharding import PartitionSpec as P

MESH = pl.DeviceIdType.MESH
VELOCITY = (
    (0, 0, 0),
    (1, 0, 0),
    (-1, 0, 0),
    (0, 1, 0),
    (0, -1, 0),
    (0, 0, 1),
    (0, 0, -1),
    (1, 1, 0),
    (-1, -1, 0),
    (1, -1, 0),
    (-1, 1, 0),
    (1, 0, 1),
    (-1, 0, -1),
    (1, 0, -1),
    (-1, 0, 1),
    (0, 1, 1),
    (0, -1, -1),
    (0, 1, -1),
    (0, -1, 1),
)
YP = (3, 7, 10, 15, 17)
YM = (4, 8, 9, 16, 18)
ZP = (5, 11, 14, 15, 18)
ZM = (6, 12, 13, 16, 17)
ORDER = YP + YM + (0, 1, 2, 5, 6, 11, 12, 13, 14)
SLOT = tuple(ORDER.index(comp) for comp in range(19))
EDGES = ((15, 1, 1), (16, -1, -1), (17, -1, 1), (18, 1, -1))
BODY_FORCE = 0.01
GRAINS = 16


def swap_groups(values, axis, size):
    values = list(values)
    length = values[0].shape[axis]
    group = lax.broadcasted_iota(jnp.int32, values[0].shape, axis) // size
    for bit in (1, 2, 4):
        upper = (group & bit) != 0
        for i in range(8):
            if i & bit == 0:
                low, high = values[i], values[i + bit]
                values[i] = jnp.where(upper, pltpu.roll(high, size * bit, axis), low)
                values[i + bit] = jnp.where(upper, high, pltpu.roll(low, length - size * bit, axis))
    return values


def collide(g, solid):
    dif = {i: g[i] - g[i + 1] for i in range(1, 19, 2)}
    add = {i: g[i] + g[i + 1] for i in range(1, 19, 2)}
    axes = add[1] + add[3] + add[5]
    diag = (add[7] + add[9]) + (add[11] + add[13]) + (add[15] + add[17])
    dens = 12.0 * g[0] + 2.0 * axes + diag
    mom_x = 2.0 * dif[1] + ((dif[7] + dif[9]) + (dif[11] + dif[13]))
    mom_y = 2.0 * dif[3] + ((dif[7] - dif[9]) + (dif[15] + dif[17]))
    mom_z = 2.0 * dif[5] + ((dif[11] - dif[13]) + (dif[15] - dif[17]))
    inv = 1.0 / dens
    ux = (mom_x + 18.0 * BODY_FORCE) * inv
    uy = mom_y * inv
    uz = mom_z * inv
    scaled = dens * (1.25 / 36.0)
    base = scaled * (1.0 - 1.5 * (ux * ux + uy * uy + uz * uz))
    square = 4.5 * scaled
    linear = 3.0 * scaled
    along = {
        1: ux,
        3: uy,
        5: uz,
        7: ux + uy,
        9: ux - uy,
        11: ux + uz,
        13: ux - uz,
        15: uy + uz,
        17: uy - uz,
    }
    posts = [None] * 19
    relaxed = base - 0.25 * g[0]
    posts[0] = relaxed + solid * (g[0] - relaxed)
    for i, a in along.items():
        even = base + square * (a * a)
        odd = linear * a
        if VELOCITY[i][0]:
            odd = odd + 3.0 * BODY_FORCE
        plus = even + odd - 0.25 * g[i]
        minus = even - odd - 0.25 * g[i + 1]
        posts[i] = plus + solid * (g[i + 1] - plus)
        posts[i + 1] = minus + solid * (g[i] - minus)
    return posts


def streamed(buf, comp, y):
    vx, vy, vz = VELOCITY[comp]
    value = buf[SLOT[comp], y + 1 - vy, 8 - vz : 24 - vz, :]
    if vx:
        value = pltpu.roll(value, vx % 128, 1)
    return value


def kernel(
    ngx, ngy,
    angle, phase, solute, grain, flags, pops,
    phase_out, solute_out, out,
    pv, ysend, yrecv, xrecv, tsend, trecv, solid_p, s1, s2, zsend, zrecv, csend, crecv,
    pop_sem, fs_sem, fr_sem, ts_sem, tr_sem, ls_sem, lr_sem,
):
    me_x, me_y = lax.axis_index("gx"), lax.axis_index("gy")

    def dev(dx, dy):
        return {"gx": lax.rem(me_x + dx + ngx, ngx), "gy": lax.rem(me_y + dy + ngy, ngy)}

    def remote(src, dst, send, recv, device):
        copy = pltpu.make_async_remote_copy(
            src_ref=src, dst_ref=dst, send_sem=send, recv_sem=recv, device_id=device, device_id_type=MESH
        )
        copy.start()
        return copy

    partners = [dev(d, 0) for d in range(1, ngx)] + [dev(0, 1), dev(0, -1)]
    partners += [dev(dx, dy) for _, dx, dy in EDGES]
    barrier = pltpu.get_barrier_semaphore()
    for device in partners:
        pl.semaphore_signal(barrier, inc=1, device_id=device, device_id_type=MESH)
    pop_copy = pltpu.make_async_copy(pops, pv, pop_sem)
    pop_copy.start()
    for field, ref in enumerate((phase, solute)):
        ysend[0, field] = ref[:, 7, :]
        ysend[1, field] = ref[:, 0, :]
    pl.semaphore_wait(barrier, len(partners))

    faces = []
    for side, step in ((0, 1), (1, -1)):
        faces.append(remote(ysend.at[side], yrecv.at[side], fs_sem.at[side], fr_sem.at[side], dev(0, step)))
    for side, step, layer in ((0, 1, 7), (1, -1, 0)):
        for field, ref in enumerate((phase, solute)):
            n = 2 + 2 * side + field
            faces.append(remote(ref.at[layer], xrecv.at[side, field], fs_sem.at[n], fr_sem.at[n], dev(step, 0)))

    lane = lax.broadcasted_iota(jnp.int32, (8, 128), 1)
    table = jnp.zeros((8, 128), jnp.float32)
    for which in range(GRAINS):
        table = jnp.where(lane == which, angle[which], table)
    cos_table, sin_table = jnp.cos(4.0 * table), jnp.sin(4.0 * table)
    cos_of = [jnp.broadcast_to(cos_table[:, i : i + 1], (8, 256)) for i in range(GRAINS)]
    sin_of = [jnp.broadcast_to(sin_table[:, i : i + 1], (8, 256)) for i in range(GRAINS)]
    cos_cell, sin_cell = [], []
    for x in range(8):
        ids = grain[x]
        c, s = cos_of, sin_of
        for bit in (1, 2, 4, 8):
            on = (ids & bit) != 0
            c = [jnp.where(on, c[2 * i + 1], c[2 * i]) for i in range(len(c) // 2)]
            s = [jnp.where(on, s[2 * i + 1], s[2 * i]) for i in range(len(s) // 2)]
        cos_cell.append(c[0])
        sin_cell.append(s[0])

    open_row = jnp.concatenate([flags[y : y + 1, :] for y in range(8)], axis=1)

    for copy in faces:
        copy.wait_recv()
    row = lax.broadcasted_iota(jnp.int32, (8, 256), 0)

    def around(ref, field, x):
        value = ref[x]
        xplus = ref[x + 1] if x < 7 else xrecv[1, field]
        xminus = ref[x - 1] if x > 0 else xrecv[0, field]
        yplus = jnp.where(row == 7, yrecv[1, field, x : x + 1, :], pltpu.roll(value, 7, 0))
        yminus = jnp.where(row == 0, yrecv[0, field, x : x + 1, :], pltpu.roll(value, 1, 0))
        zplus, zminus = pltpu.roll(value, 255, 1), pltpu.roll(value, 1, 1)
        laplace = (xplus + xminus) + (yplus + yminus) + (zplus + zminus) - 6.0 * value
        return value, laplace, xplus - xminus, yplus - yminus

    solids = []
    for x in range(8):
        ph, lap, dx, dy = around(phase, 0, x)
        so, lap_so, _, _ = around(solute, 1, x)
        gx, gy = 0.5 * dx, 0.5 * dy
        sx, sy = gx * gx, gy * gy
        denom = sx + sy + 0.25
        inv = 1.0 / (denom * denom)
        cos_four = (sx * sx - 6.0 * sx * sy + sy * sy) * inv
        sin_four = 4.0 * gx * gy * (sx - sy) * inv
        aniso = 1.0 + 0.3 * (cos_four * cos_cell[x] + sin_four * sin_cell[x])
        bulk = 1.0 - ph * ph
        change = 0.08 * aniso * aniso * (lap + ph - ph * ph * ph - 1.5 * so * bulk * bulk)
        ph_next = ph + change
        phase_out[x] = ph_next
        solute_out[x] = so + 0.16 * lap_so + 0.5 * (ph_next - ph)
        solids.append(jnp.clip(0.5 * (1.0 + ph_next), 0.0, 1.0))

    rows = swap_groups(solids, 0, 1)
    for half in range(2):
        tiles = swap_groups([r[:, 128 * half : 128 * half + 128] for r in rows], 1, 16)
        for j in range(8):
            tsend[8 * half + j] = tiles[j]
    moves = []
    for d in range(1, ngx):
        device = dev(d, 0)
        moves.append(
            remote(tsend.at[device["gx"]], trecv.at[me_x], ts_sem.at[d - 1], tr_sem.at[d - 1], device)
        )
    trecv[me_x] = tsend[me_x]
    pop_copy.wait()
    for copy in moves:
        copy.wait_recv()
    whole = trecv[...].reshape(128, 128)
    first = lax.broadcasted_iota(jnp.int32, (128, 128), 0) == 0
    whole = jnp.where(first & (open_row == 0), 1.0, whole)
    solid_p[...] = jnp.transpose(whole).reshape(8, 16, 128)

    pending = []

    def step(which, buf, source):
        def one(t, carry):
            y = lax.rem(t + 7, 8)
            posts = collide(source(y), solid_p[y])
            for comp in range(19):
                buf[SLOT[comp], y + 1, 8:24, :] = posts[comp]
            return carry

        sems = lambda n: (ls_sem.at[which, n], lr_sem.at[which, n])
        lax.fori_loop(0, 2, one, 0)
        copies = [
            remote(buf.at[0:5, 8, 8:24], buf.at[0:5, 0, 8:24], *sems(0), dev(0, 1)),
            remote(buf.at[5:10, 1, 8:24], buf.at[5:10, 9, 8:24], *sems(1), dev(0, -1)),
        ]
        for n, (comp, dx, dy) in enumerate(EDGES):
            y, z = (8 if dy > 0 else 1), (23 if dx > 0 else 8)
            csend[which, n, 0:1] = buf[SLOT[comp], y, z : z + 1, :]
            copies.append(remote(csend.at[which, n], crecv.at[which, n], *sems(2 + n), dev(dx, dy)))
        lax.fori_loop(2, 8, one, 0)
        for side, comps, z, dx in ((0, ZP, 23, 1), (1, ZM, 8, -1)):
            for n, comp in enumerate(comps):
                zsend[which, side, n] = buf[SLOT[comp], 1:9, z, :]
            copies.append(remote(zsend.at[which, side], zrecv.at[which, side], *sems(6 + side), dev(dx, 0)))
        for copy in copies:
            copy.wait_recv()
        pending.extend(copies)
        for side, comps, z in ((0, ZP, 7), (1, ZM, 24)):
            for n, comp in enumerate(comps):
                buf[SLOT[comp], 1:9, z, :] = zrecv[which, side, n]
        for n, (comp, dx, dy) in enumerate(EDGES):
            y, z = (0 if dy > 0 else 9), (7 if dx > 0 else 24)
            buf[SLOT[comp], y, z : z + 1, :] = crecv[which, n, 0:1]

    step(0, s1, lambda y: [pv[comp, y] for comp in range(19)])
    step(1, s2, lambda y: [streamed(s1, comp, y) for comp in range(19)])

    def last(y, carry):
        for comp in range(19):
            out[comp, y] = streamed(s2, comp, y)
        return carry

    lax.fori_loop(0, 8, last, 0)
    for copy in faces + moves + pending:
        copy.wait_send()


def per_device(ngx, ngy, phase, solute, grain, grain_angle, inlet_flags, populations):
    vmem = pl.BlockSpec(memory_space=pltpu.VMEM)
    return pl.pallas_call(
        functools.partial(kernel, ngx, ngy),
        out_shape=[
            jax.ShapeDtypeStruct(phase.shape, jnp.float32),
            jax.ShapeDtypeStruct(solute.shape, jnp.float32),
            jax.ShapeDtypeStruct(populations.shape, jnp.float32),
        ],
        in_specs=[pl.BlockSpec(memory_space=pltpu.SMEM), vmem, vmem, vmem, vmem, pl.BlockSpec(memory_space=pl.ANY)],
        out_specs=[vmem, vmem, vmem],
        scratch_shapes=[
            pltpu.VMEM((19, 8, 16, 128), jnp.float32),
            pltpu.VMEM((2, 2, 8, 256), jnp.float32),
            pltpu.VMEM((2, 2, 8, 256), jnp.float32),
            pltpu.VMEM((2, 2, 8, 256), jnp.float32),
            pltpu.VMEM((ngx, 8, 128), jnp.float32),
            pltpu.VMEM((ngx, 8, 128), jnp.float32),
            pltpu.VMEM((8, 16, 128), jnp.float32),
            pltpu.VMEM((19, 10, 32, 128), jnp.float32),
            pltpu.VMEM((19, 10, 32, 128), jnp.float32),
            pltpu.VMEM((2, 2, 5, 8, 128), jnp.float32),
            pltpu.VMEM((2, 2, 5, 8, 128), jnp.float32),
            pltpu.VMEM((2, 4, 8, 128), jnp.float32),
            pltpu.VMEM((2, 4, 8, 128), jnp.float32),
            pltpu.SemaphoreType.DMA,
            pltpu.SemaphoreType.DMA((6,)),
            pltpu.SemaphoreType.DMA((6,)),
            pltpu.SemaphoreType.DMA((ngx - 1,)),
            pltpu.SemaphoreType.DMA((ngx - 1,)),
            pltpu.SemaphoreType.DMA((2, 8)),
            pltpu.SemaphoreType.DMA((2, 8)),
        ],
        compiler_params=pltpu.CompilerParams(
            collective_id=0, has_side_effects=True, vmem_limit_bytes=40 * 1024 * 1024
        ),
    )(grain_angle, phase, solute, grain, inlet_flags, populations)


def solution(mesh):
    return jax.shard_map(
        functools.partial(per_device, mesh.shape["gx"], mesh.shape["gy"]),
        mesh=mesh,
        in_specs=(
            P("gx", "gy", None),
            P("gx", "gy", None),
            P("gx", "gy", None),
            P(),
            P("gy", "gx"),
            P(None, "gy", "gx", None),
        ),
        out_specs=(P("gx", "gy", None), P("gx", "gy", None), P(None, "gy", "gx", None)),
        check_vma=False,
    )
```

```python
import functools

import jax
import jax.numpy as jnp
from jax import lax
from jax.experimental import pallas as pl
from jax.experimental.pallas import tpu as pltpu
from jax.sharding import PartitionSpec as P

MESH = pl.DeviceIdType.MESH
VELOCITY = (
    (0, 0, 0),
    (1, 0, 0),
    (-1, 0, 0),
    (0, 1, 0),
    (0, -1, 0),
    (0, 0, 1),
    (0, 0, -1),
    (1, 1, 0),
    (-1, -1, 0),
    (1, -1, 0),
    (-1, 1, 0),
    (1, 0, 1),
    (-1, 0, -1),
    (1, 0, -1),
    (-1, 0, 1),
    (0, 1, 1),
    (0, -1, -1),
    (0, 1, -1),
    (0, -1, 1),
)
YP = (3, 7, 10, 15, 17)
YM = (4, 8, 9, 16, 18)
ZP = (5, 11, 14, 15, 18)
ZM = (6, 12, 13, 16, 17)
ORDER = YP + YM + (0, 1, 2, 5, 6, 11, 12, 13, 14)
SLOT = tuple(ORDER.index(comp) for comp in range(19))
EDGES = ((15, 1, 1), (16, -1, -1), (17, -1, 1), (18, 1, -1))
BODY_FORCE = 0.01
GRAINS = 16


def swap_groups(values, axis, size):
    values = list(values)
    length = values[0].shape[axis]
    group = lax.broadcasted_iota(jnp.int32, values[0].shape, axis) // size
    for bit in (1, 2, 4):
        upper = (group & bit) != 0
        for i in range(8):
            if i & bit == 0:
                low, high = values[i], values[i + bit]
                values[i] = jnp.where(upper, pltpu.roll(high, size * bit, axis), low)
                values[i + bit] = jnp.where(upper, high, pltpu.roll(low, length - size * bit, axis))
    return values


def collide(g, solid):
    dif = {i: g[i] - g[i + 1] for i in range(1, 19, 2)}
    add = {i: g[i] + g[i + 1] for i in range(1, 19, 2)}
    axes = add[1] + add[3] + add[5]
    diag = (add[7] + add[9]) + (add[11] + add[13]) + (add[15] + add[17])
    dens = 12.0 * g[0] + 2.0 * axes + diag
    mom_x = 2.0 * dif[1] + ((dif[7] + dif[9]) + (dif[11] + dif[13]))
    mom_y = 2.0 * dif[3] + ((dif[7] - dif[9]) + (dif[15] + dif[17]))
    mom_z = 2.0 * dif[5] + ((dif[11] - dif[13]) + (dif[15] - dif[17]))
    inv = 1.0 / dens
    ux = (mom_x + 18.0 * BODY_FORCE) * inv
    uy = mom_y * inv
    uz = mom_z * inv
    scaled = dens * (1.25 / 36.0)
    base = scaled * (1.0 - 1.5 * (ux * ux + uy * uy + uz * uz))
    square = 4.5 * scaled
    linear = 3.0 * scaled
    along = {
        1: ux,
        3: uy,
        5: uz,
        7: ux + uy,
        9: ux - uy,
        11: ux + uz,
        13: ux - uz,
        15: uy + uz,
        17: uy - uz,
    }
    posts = [None] * 19
    relaxed = base - 0.25 * g[0]
    posts[0] = relaxed + solid * (g[0] - relaxed)
    for i, a in along.items():
        even = base + square * (a * a)
        odd = linear * a
        if VELOCITY[i][0]:
            odd = odd + 3.0 * BODY_FORCE
        plus = even + odd - 0.25 * g[i]
        minus = even - odd - 0.25 * g[i + 1]
        posts[i] = plus + solid * (g[i + 1] - plus)
        posts[i + 1] = minus + solid * (g[i] - minus)
    return posts


def streamed(buf, comp, y):
    vx, vy, vz = VELOCITY[comp]
    value = buf[SLOT[comp], y + 1 - vy, 8 - vz : 24 - vz, :]
    if vx:
        value = pltpu.roll(value, vx % 128, 1)
    return value


def kernel(
    ngx, ngy,
    angle_in, phase_in, solute_in, grain_in, flags_in, pops,
    phase_out, solute_out, s2,
    angle, phase, solute, grain, flags, pv, ysend, yrecv, xrecv, tsend, trecv, solid_p, s1, zsend, zrecv, csend, crecv,
    in_sem, fs_sem, fr_sem, ts_sem, tr_sem, ls_sem, lr_sem,
):
    me_x, me_y = lax.axis_index("gx"), lax.axis_index("gy")

    def dev(dx, dy):
        return {"gx": lax.rem(me_x + dx + ngx, ngx), "gy": lax.rem(me_y + dy + ngy, ngy)}

    def remote(src, dst, send, recv, device):
        copy = pltpu.make_async_remote_copy(
            src_ref=src, dst_ref=dst, send_sem=send, recv_sem=recv, device_id=device, device_id_type=MESH
        )
        copy.start()
        return copy

    loads = []
    for n, (src, dst) in enumerate(
        ((phase_in, phase), (solute_in, solute), (angle_in, angle), (grain_in, grain), (flags_in, flags), (pops, pv))
    ):
        loads.append(pltpu.make_async_copy(src, dst, in_sem.at[n]))
        loads[-1].start()
    partners = [dev(d, 0) for d in range(1, ngx)] + [dev(0, 1), dev(0, -1)]
    partners += [dev(dx, dy) for _, dx, dy in EDGES]
    barrier = pltpu.get_barrier_semaphore()
    for device in partners:
        pl.semaphore_signal(barrier, inc=1, device_id=device, device_id_type=MESH)
    loads[0].wait()
    loads[1].wait()
    for field, ref in enumerate((phase, solute)):
        ysend[0, field] = ref[:, 7, :]
        ysend[1, field] = ref[:, 0, :]
    pl.semaphore_wait(barrier, len(partners))

    faces = []
    for side, step in ((0, 1), (1, -1)):
        faces.append(remote(ysend.at[side], yrecv.at[side], fs_sem.at[side], fr_sem.at[side], dev(0, step)))
    for side, step, layer in ((0, 1, 7), (1, -1, 0)):
        for field, ref in enumerate((phase, solute)):
            n = 2 + 2 * side + field
            faces.append(remote(ref.at[layer], xrecv.at[side, field], fs_sem.at[n], fr_sem.at[n], dev(step, 0)))

    loads[2].wait()
    lane = lax.broadcasted_iota(jnp.int32, (8, 128), 1)
    table = jnp.zeros((8, 128), jnp.float32)
    for which in range(GRAINS):
        table = jnp.where(lane == which, angle[which], table)
    cos_table, sin_table = jnp.cos(4.0 * table), jnp.sin(4.0 * table)
    cos_of = [jnp.broadcast_to(cos_table[:, i : i + 1], (8, 256)) for i in range(GRAINS)]
    sin_of = [jnp.broadcast_to(sin_table[:, i : i + 1], (8, 256)) for i in range(GRAINS)]
    cos_cell, sin_cell = [], []
    loads[3].wait()
    for x in range(8):
        ids = grain[x]
        c, s = cos_of, sin_of
        for bit in (1, 2, 4, 8):
            on = (ids & bit) != 0
            c = [jnp.where(on, c[2 * i + 1], c[2 * i]) for i in range(len(c) // 2)]
            s = [jnp.where(on, s[2 * i + 1], s[2 * i]) for i in range(len(s) // 2)]
        cos_cell.append(c[0])
        sin_cell.append(s[0])

    loads[4].wait()
    open_row = jnp.concatenate([flags[y : y + 1, :] for y in range(8)], axis=1)

    for copy in faces:
        copy.wait_recv()
    row = lax.broadcasted_iota(jnp.int32, (8, 256), 0)

    def around(ref, field, x):
        value = ref[x]
        xplus = ref[x + 1] if x < 7 else xrecv[1, field]
        xminus = ref[x - 1] if x > 0 else xrecv[0, field]
        yplus = jnp.where(row == 7, yrecv[1, field, x : x + 1, :], pltpu.roll(value, 7, 0))
        yminus = jnp.where(row == 0, yrecv[0, field, x : x + 1, :], pltpu.roll(value, 1, 0))
        zplus, zminus = pltpu.roll(value, 255, 1), pltpu.roll(value, 1, 1)
        laplace = (xplus + xminus) + (yplus + yminus) + (zplus + zminus) - 6.0 * value
        return value, laplace, xplus - xminus, yplus - yminus

    solids = []
    for x in range(8):
        ph, lap, dx, dy = around(phase, 0, x)
        so, lap_so, _, _ = around(solute, 1, x)
        gx, gy = 0.5 * dx, 0.5 * dy
        sx, sy = gx * gx, gy * gy
        denom = sx + sy + 0.25
        inv = 1.0 / (denom * denom)
        cos_four = (sx * sx - 6.0 * sx * sy + sy * sy) * inv
        sin_four = 4.0 * gx * gy * (sx - sy) * inv
        aniso = 1.0 + 0.3 * (cos_four * cos_cell[x] + sin_four * sin_cell[x])
        bulk = 1.0 - ph * ph
        change = 0.08 * aniso * aniso * (lap + ph - ph * ph * ph - 1.5 * so * bulk * bulk)
        ph_next = ph + change
        phase_out[x] = ph_next
        solute_out[x] = so + 0.16 * lap_so + 0.5 * (ph_next - ph)
        solids.append(jnp.clip(0.5 * (1.0 + ph_next), 0.0, 1.0))

    rows = swap_groups(solids, 0, 1)
    for half in range(2):
        tiles = swap_groups([r[:, 128 * half : 128 * half + 128] for r in rows], 1, 16)
        for j in range(8):
            tsend[8 * half + j] = tiles[j]
    moves = []
    for d in range(1, ngx):
        device = dev(d, 0)
        moves.append(
            remote(tsend.at[device["gx"]], trecv.at[me_x], ts_sem.at[d - 1], tr_sem.at[d - 1], device)
        )
    trecv[me_x] = tsend[me_x]
    loads[5].wait()
    for copy in moves:
        copy.wait_recv()
    whole = trecv[...].reshape(128, 128)
    first = lax.broadcasted_iota(jnp.int32, (128, 128), 0) == 0
    whole = jnp.where(first & (open_row == 0), 1.0, whole)
    solid_p[...] = jnp.transpose(whole).reshape(8, 16, 128)

    pending = []

    def step(which, buf, source):
        def one(t, carry):
            y = lax.rem(t + 7, 8)
            posts = collide(source(y), solid_p[y])
            for comp in range(19):
                buf[SLOT[comp], y + 1, 8:24, :] = posts[comp]
            return carry

        sems = lambda n: (ls_sem.at[which, n], lr_sem.at[which, n])
        lax.fori_loop(0, 2, one, 0)
        copies = [
            remote(buf.at[0:5, 8, 8:24], buf.at[0:5, 0, 8:24], *sems(0), dev(0, 1)),
            remote(buf.at[5:10, 1, 8:24], buf.at[5:10, 9, 8:24], *sems(1), dev(0, -1)),
        ]
        for n, (comp, dx, dy) in enumerate(EDGES):
            y, z = (8 if dy > 0 else 1), (23 if dx > 0 else 8)
            csend[which, n, 0:1] = buf[SLOT[comp], y, z : z + 1, :]
            copies.append(remote(csend.at[which, n], crecv.at[which, n], *sems(2 + n), dev(dx, dy)))
        lax.fori_loop(2, 8, one, 0)
        for side, comps, z, dx in ((0, ZP, 23, 1), (1, ZM, 8, -1)):
            for n, comp in enumerate(comps):
                zsend[which, side, n] = buf[SLOT[comp], 1:9, z, :]
            copies.append(remote(zsend.at[which, side], zrecv.at[which, side], *sems(6 + side), dev(dx, 0)))
        for copy in copies:
            copy.wait_recv()
        pending.extend(copies)
        for side, comps, z in ((0, ZP, 7), (1, ZM, 24)):
            for n, comp in enumerate(comps):
                buf[SLOT[comp], 1:9, z, :] = zrecv[which, side, n]
        for n, (comp, dx, dy) in enumerate(EDGES):
            y, z = (0 if dy > 0 else 9), (7 if dx > 0 else 24)
            buf[SLOT[comp], y, z : z + 1, :] = crecv[which, n, 0:1]

    step(0, s1, lambda y: [pv[comp, y] for comp in range(19)])
    step(1, s2, lambda y: [streamed(s1, comp, y) for comp in range(19)])

    for copy in faces + moves + pending:
        copy.wait_send()


def finish(phase_next, solute_next, s2, phase_out, solute_out, out, buf, sems):
    copies = [
        pltpu.make_async_copy(phase_next, phase_out, sems.at[8]),
        pltpu.make_async_copy(solute_next, solute_out, sems.at[9]),
    ]
    for copy in copies:
        copy.start()
    for y in range(8):
        for comp in range(19):
            buf[comp, y] = streamed(s2, comp, y)
        copies.append(pltpu.make_async_copy(buf.at[:, y], out.at[:, y], sems.at[y]))
        copies[-1].start()
    for copy in copies:
        copy.wait()


def per_device(ngx, ngy, phase, solute, grain, grain_angle, inlet_flags, populations):
    vmem = pl.BlockSpec(memory_space=pltpu.VMEM)
    operands = (grain_angle, phase, solute, grain, inlet_flags, populations)
    hbm = pl.BlockSpec(memory_space=pltpu.HBM)
    phase_next, solute_next, s2 = pl.pallas_call(
        functools.partial(kernel, ngx, ngy),
        out_shape=[
            jax.ShapeDtypeStruct(phase.shape, jnp.float32),
            jax.ShapeDtypeStruct(solute.shape, jnp.float32),
            jax.ShapeDtypeStruct((19, 10, 32, 128), jnp.float32),
        ],
        in_specs=[hbm] * 6,
        out_specs=[vmem, vmem, vmem],
        scratch_shapes=[
            pltpu.SMEM((16,), jnp.float32),
            pltpu.VMEM((8, 8, 256), jnp.float32),
            pltpu.VMEM((8, 8, 256), jnp.float32),
            pltpu.VMEM((8, 8, 256), jnp.int32),
            pltpu.VMEM((8, 16), jnp.int32),
            pltpu.VMEM((19, 8, 16, 128), jnp.float32),
            pltpu.VMEM((2, 2, 8, 256), jnp.float32),
            pltpu.VMEM((2, 2, 8, 256), jnp.float32),
            pltpu.VMEM((2, 2, 8, 256), jnp.float32),
            pltpu.VMEM((ngx, 8, 128), jnp.float32),
            pltpu.VMEM((ngx, 8, 128), jnp.float32),
            pltpu.VMEM((8, 16, 128), jnp.float32),
            pltpu.VMEM((19, 10, 32, 128), jnp.float32),
            pltpu.VMEM((2, 2, 5, 8, 128), jnp.float32),
            pltpu.VMEM((2, 2, 5, 8, 128), jnp.float32),
            pltpu.VMEM((2, 4, 8, 128), jnp.float32),
            pltpu.VMEM((2, 4, 8, 128), jnp.float32),
            pltpu.SemaphoreType.DMA((6,)),
            pltpu.SemaphoreType.DMA((6,)),
            pltpu.SemaphoreType.DMA((6,)),
            pltpu.SemaphoreType.DMA((ngx - 1,)),
            pltpu.SemaphoreType.DMA((ngx - 1,)),
            pltpu.SemaphoreType.DMA((2, 8)),
            pltpu.SemaphoreType.DMA((2, 8)),
        ],
        compiler_params=pltpu.CompilerParams(
            collective_id=0, has_side_effects=True, vmem_limit_bytes=40 * 1024 * 1024
        ),
    )(*[pltpu.with_memory_space_constraint(a, pltpu.HBM) for a in operands])
    return pl.pallas_call(
        finish,
        out_shape=[
            jax.ShapeDtypeStruct(phase.shape, jnp.float32),
            jax.ShapeDtypeStruct(solute.shape, jnp.float32),
            jax.ShapeDtypeStruct(populations.shape, jnp.float32),
        ],
        in_specs=[vmem] * 3,
        out_specs=[hbm] * 3,
        scratch_shapes=[pltpu.VMEM((19, 8, 16, 128), jnp.float32), pltpu.SemaphoreType.DMA((10,))],
        compiler_params=pltpu.CompilerParams(vmem_limit_bytes=40 * 1024 * 1024),
    )(phase_next, solute_next, s2)


def solution(mesh):
    return jax.shard_map(
        functools.partial(per_device, mesh.shape["gx"], mesh.shape["gy"]),
        mesh=mesh,
        in_specs=(
            P("gx", "gy", None),
            P("gx", "gy", None),
            P("gx", "gy", None),
            P(),
            P("gy", "gx"),
            P(None, "gy", "gx", None),
        ),
        out_specs=(P("gx", "gy", None), P("gx", "gy", None), P(None, "gy", "gx", None)),
        check_vma=False,
    )
```

```python
import functools

import jax
import jax.numpy as jnp
from jax import lax
from jax.experimental import pallas as pl
from jax.experimental.pallas import tpu as pltpu
from jax.sharding import PartitionSpec as P

MESH = pl.DeviceIdType.MESH
VELOCITY = (
    (0, 0, 0),
    (1, 0, 0),
    (-1, 0, 0),
    (0, 1, 0),
    (0, -1, 0),
    (0, 0, 1),
    (0, 0, -1),
    (1, 1, 0),
    (-1, -1, 0),
    (1, -1, 0),
    (-1, 1, 0),
    (1, 0, 1),
    (-1, 0, -1),
    (1, 0, -1),
    (-1, 0, 1),
    (0, 1, 1),
    (0, -1, -1),
    (0, 1, -1),
    (0, -1, 1),
)
YP = (3, 7, 10, 15, 17)
YM = (4, 8, 9, 16, 18)
ZP = (5, 11, 14, 15, 18)
ZM = (6, 12, 13, 16, 17)
ORDER = YP + YM + (0, 1, 2, 5, 6, 11, 12, 13, 14)
SLOT = tuple(ORDER.index(comp) for comp in range(19))
EDGES = ((15, 1, 1), (16, -1, -1), (17, -1, 1), (18, 1, -1))
OPPOSITE = (0, 2, 1, 4, 3, 6, 5, 8, 7, 10, 9, 12, 11, 14, 13, 16, 15, 18, 17)
BODY_FORCE = 0.01
GRAINS = 16


def swap_groups(values, axis, size):
    values = list(values)
    length = values[0].shape[axis]
    group = lax.broadcasted_iota(jnp.int32, values[0].shape, axis) // size
    for bit in (1, 2, 4):
        upper = (group & bit) != 0
        for i in range(8):
            if i & bit == 0:
                low, high = values[i], values[i + bit]
                values[i] = jnp.where(upper, pltpu.roll(high, size * bit, axis), low)
                values[i + bit] = jnp.where(upper, high, pltpu.roll(low, length - size * bit, axis))
    return values


def relax(g):
    dif = {i: g[i] - g[i + 1] for i in range(1, 19, 2)}
    add = {i: g[i] + g[i + 1] for i in range(1, 19, 2)}
    axes = add[1] + add[3] + add[5]
    diag = (add[7] + add[9]) + (add[11] + add[13]) + (add[15] + add[17])
    dens = 12.0 * g[0] + 2.0 * axes + diag
    mom_x = 2.0 * dif[1] + ((dif[7] + dif[9]) + (dif[11] + dif[13]))
    mom_y = 2.0 * dif[3] + ((dif[7] - dif[9]) + (dif[15] + dif[17]))
    mom_z = 2.0 * dif[5] + ((dif[11] - dif[13]) + (dif[15] - dif[17]))
    inv = 1.0 / dens
    ux = (mom_x + 18.0 * BODY_FORCE) * inv
    uy = mom_y * inv
    uz = mom_z * inv
    scaled = dens * (1.25 / 36.0)
    base = scaled * (1.0 - 1.5 * (ux * ux + uy * uy + uz * uz))
    square = 4.5 * scaled
    linear = 3.0 * scaled
    along = {
        1: ux,
        3: uy,
        5: uz,
        7: ux + uy,
        9: ux - uy,
        11: ux + uz,
        13: ux - uz,
        15: uy + uz,
        17: uy - uz,
    }
    relaxed = [None] * 19
    relaxed[0] = base - 0.25 * g[0]
    for i, a in along.items():
        even = base + square * (a * a)
        odd = linear * a
        if VELOCITY[i][0]:
            odd = odd + 3.0 * BODY_FORCE
        relaxed[i] = even + odd - 0.25 * g[i]
        relaxed[i + 1] = even - odd - 0.25 * g[i + 1]
    return relaxed


def blend(relaxed, back, solid):
    return relaxed + solid * (back - relaxed)


def next_phase(ph, lap, dx, dy, so, cos_cell, sin_cell):
    gx, gy = 0.5 * dx, 0.5 * dy
    sx, sy = gx * gx, gy * gy
    denom = sx + sy + 0.25
    inv = 1.0 / (denom * denom)
    cos_four = (sx * sx - 6.0 * sx * sy + sy * sy) * inv
    sin_four = 4.0 * gx * gy * (sx - sy) * inv
    aniso = 1.0 + 0.3 * (cos_four * cos_cell + sin_four * sin_cell)
    bulk = 1.0 - ph * ph
    return ph + 0.08 * aniso * aniso * (lap + ph - ph * ph * ph - 1.5 * so * bulk * bulk)


def solid_of(ph):
    return jnp.clip(0.5 * (1.0 + ph), 0.0, 1.0)


def streamed(buf, comp, y):
    vx, vy, vz = VELOCITY[comp]
    value = buf[SLOT[comp], y + 1 - vy, 8 - vz : 24 - vz, :]
    if vx:
        value = pltpu.roll(value, vx % 128, 1)
    return value


def kernel(
    ngx, ngy,
    angle_in, phase_in, solute_in, grain_in, flags_in, pops,
    phase_out, solute_out, s2,
    angle, phase, solute, grain, flags, pv, rel, ysend, yrecv, xrecv, dsend, drecv,
    tsend, trecv, solid_p, closed, solid_z, solid_h, s1,
    yab, yab_in, zab, zab_in, cab, cab_in, zsend, zrecv, csend, crecv,
    in_sem, fs_sem, fr_sem, bs_sem, br_sem, ts_sem, tr_sem, ls_sem, lr_sem,
):
    me_x, me_y = lax.axis_index("gx"), lax.axis_index("gy")

    def dev(dx, dy):
        return {"gx": lax.rem(me_x + dx + ngx, ngx), "gy": lax.rem(me_y + dy + ngy, ngy)}

    def remote(src, dst, send, recv, device):
        copy = pltpu.make_async_remote_copy(
            src_ref=src, dst_ref=dst, send_sem=send, recv_sem=recv, device_id=device, device_id_type=MESH
        )
        copy.start()
        return copy

    loads = []
    for n, (src, dst) in enumerate(
        ((phase_in, phase), (solute_in, solute), (angle_in, angle), (grain_in, grain), (flags_in, flags), (pops, pv))
    ):
        loads.append(pltpu.make_async_copy(src, dst, in_sem.at[n]))
        loads[-1].start()
    partners = [dev(d, 0) for d in range(1, ngx)] + [dev(0, 1), dev(0, -1)]
    partners += [dev(dx, dy) for _, dx, dy in EDGES]
    barrier = pltpu.get_barrier_semaphore()
    for device in partners:
        pl.semaphore_signal(barrier, inc=1, device_id=device, device_id_type=MESH)
    loads[0].wait()
    loads[1].wait()
    loads[3].wait()
    for side, edge, second in ((0, 7, 6), (1, 0, 1)):
        ysend[side, 0] = phase[:, edge, :]
        ysend[side, 1] = phase[:, second, :]
        ysend[side, 2] = solute[:, edge, :]
        ysend[side, 3] = grain[:, edge, :].astype(jnp.float32)
    for n, (_, dx, dy) in enumerate(EDGES):
        line = phase[7 if dx > 0 else 0, 7 if dy > 0 else 0 : 8 if dy > 0 else 1, :]
        dsend[n, 0:1] = line[:, :128]
        dsend[n, 1:2] = line[:, 128:]
    pl.semaphore_wait(barrier, len(partners))

    faces = []
    for n, (_, dx, dy) in enumerate(EDGES):
        faces.append(remote(dsend.at[n], drecv.at[n], fs_sem.at[6 + n], fr_sem.at[6 + n], dev(dx, dy)))
    for side, step, layer in ((0, 1, 7), (1, -1, 0)):
        for field, ref in enumerate((phase, solute)):
            n = 2 + 2 * side + field
            faces.append(remote(ref.at[layer], xrecv.at[side, field], fs_sem.at[n], fr_sem.at[n], dev(step, 0)))
    for side, step in ((0, 1), (1, -1)):
        faces.append(remote(ysend.at[side], yrecv.at[side], fs_sem.at[side], fr_sem.at[side], dev(0, step)))

    loads[4].wait()
    open_row = jnp.concatenate([flags[y : y + 1, :] for y in range(8)], axis=1)
    first = lax.broadcasted_iota(jnp.int32, (128, 128), 0) == 0
    closed[...] = jnp.transpose(jnp.where(first & (open_row == 0), 1.0, 0.0)).reshape(8, 16, 128)

    loads[5].wait()

    def first_relax(y, carry):
        g = [pv[comp, y] for comp in range(19)]
        shut = closed[y] > 0.5
        for comp, value in enumerate(relax(g)):
            rel[comp, y] = jnp.where(shut, g[OPPOSITE[comp]], value)
        return carry

    lax.fori_loop(0, 8, first_relax, 0)
    early = []
    for side, comps, z, dx in ((0, ZP, 15, 1), (1, ZM, 0, -1)):
        for n, comp in enumerate(comps):
            zab[side, 0, n] = rel[comp, :, z, :]
            zab[side, 1, n] = pv[OPPOSITE[comp], :, z, :]
        early.append(remote(zab.at[side], zab_in.at[side], bs_sem.at[side], br_sem.at[side], dev(dx, 0)))
    for n, (comp, dx, dy) in enumerate(EDGES):
        y, z = (7 if dy > 0 else 0), (15 if dx > 0 else 0)
        cab[n, 0:1] = rel[comp, y, z : z + 1, :]
        cab[n, 1:2] = pv[OPPOSITE[comp], y, z : z + 1, :]
        early.append(remote(cab.at[n], cab_in.at[n], bs_sem.at[4 + n], br_sem.at[4 + n], dev(dx, dy)))
    for side, comps, y in ((0, YP, 7), (1, YM, 0)):
        for n, comp in enumerate(comps):
            yab[side, 0, n] = rel[comp, y]
            yab[side, 1, n] = pv[OPPOSITE[comp], y]
    for copy in faces:
        copy.wait_send()
    for side, step in ((0, 1), (1, -1)):
        early.append(remote(yab.at[side], yab_in.at[side], bs_sem.at[2 + side], br_sem.at[2 + side], dev(0, step)))

    loads[2].wait()
    lane = lax.broadcasted_iota(jnp.int32, (8, 128), 1)
    table = jnp.zeros((8, 128), jnp.float32)
    for which in range(GRAINS):
        table = jnp.where(lane == which, angle[which], table)
    cos_table, sin_table = jnp.cos(4.0 * table), jnp.sin(4.0 * table)
    cos_of = [jnp.broadcast_to(cos_table[:, i : i + 1], (8, 256)) for i in range(GRAINS)]
    sin_of = [jnp.broadcast_to(sin_table[:, i : i + 1], (8, 256)) for i in range(GRAINS)]

    def trig(ids):
        c, s = cos_of, sin_of
        for bit in (1, 2, 4, 8):
            on = (ids & bit) != 0
            c = [jnp.where(on, c[2 * i + 1], c[2 * i]) for i in range(len(c) // 2)]
            s = [jnp.where(on, s[2 * i + 1], s[2 * i]) for i in range(len(s) // 2)]
        return c[0], s[0]

    cells = [trig(grain[x]) for x in range(8)]
    for copy in faces:
        copy.wait_recv()
    row = lax.broadcasted_iota(jnp.int32, (8, 256), 0)

    def around(ref, field, x):
        value = ref[x]
        xplus = ref[x + 1] if x < 7 else xrecv[1, field]
        xminus = ref[x - 1] if x > 0 else xrecv[0, field]
        yplus = jnp.where(row == 7, yrecv[1, 2 * field, x : x + 1, :], pltpu.roll(value, 7, 0))
        yminus = jnp.where(row == 0, yrecv[0, 2 * field, x : x + 1, :], pltpu.roll(value, 1, 0))
        zplus, zminus = pltpu.roll(value, 255, 1), pltpu.roll(value, 1, 1)
        laplace = (xplus + xminus) + (yplus + yminus) + (zplus + zminus) - 6.0 * value
        return value, laplace, xplus - xminus, yplus - yminus

    solids = []
    for x in range(8):
        ph, lap, dx, dy = around(phase, 0, x)
        so, lap_so, _, _ = around(solute, 1, x)
        ph_next = next_phase(ph, lap, dx, dy, so, *cells[x])
        phase_out[x] = ph_next
        solute_out[x] = so + 0.16 * lap_so + 0.5 * (ph_next - ph)
        solids.append(solid_of(ph_next))

    beyond = []
    for side in range(2):
        ph, second, so, ids = (yrecv[side, n] for n in range(4))
        inner = ysend[1 - side, 0]
        yplus, yminus = (inner, second) if side == 0 else (second, inner)
        lines = {}
        for n, (_, dx, dy) in enumerate(EDGES):
            if dy == (1 if side == 0 else -1):
                lines[dx] = jnp.concatenate([drecv[n, 0:1], drecv[n, 1:2]], axis=1)
        xplus = jnp.where(row == 7, lines[-1], pltpu.roll(ph, 7, 0))
        xminus = jnp.where(row == 0, lines[1], pltpu.roll(ph, 1, 0))
        lap = (xplus + xminus) + (yplus + yminus) + (pltpu.roll(ph, 255, 1) + pltpu.roll(ph, 1, 1)) - 6.0 * ph
        ph_next = next_phase(ph, lap, xplus - xminus, yplus - yminus, so, *trig(ids.astype(jnp.int32)))
        beyond.append(solid_of(ph_next))

    rows = swap_groups(solids, 0, 1)
    tiles = []
    for half in range(2):
        tiles += swap_groups([r[:, 128 * half : 128 * half + 128] for r in rows], 1, 16)
    last_lane = (lane & 15) == 15
    for k in range(ngx):
        tsend[k, 0] = tiles[k]
        tsend[k, 1] = jnp.where(last_lane, tiles[k - 1], tiles[(k + 1) % ngx])
        below = pltpu.roll(beyond[0], (272 - 16 * k) % 256, 1)[:, :128]
        above = pltpu.roll(beyond[1], (336 - 16 * k) % 256, 1)[:, :128]
        tsend[k, 2] = jnp.where(lane < 64, below, above)
    moves = []
    for d in range(1, ngx):
        device = dev(d, 0)
        moves.append(
            remote(tsend.at[device["gx"]], trecv.at[me_x], ts_sem.at[d - 1], tr_sem.at[d - 1], device)
        )
    trecv[me_x] = tsend[me_x]
    for copy in moves:
        copy.wait_recv()
    solid_p[...] = jnp.maximum(jnp.transpose(trecv[:, 0].reshape(128, 128)).reshape(8, 16, 128), closed[...])
    solid_z[...] = jnp.transpose(trecv[:, 1].reshape(128, 128)).reshape(8, 16, 128)
    solid_h[...] = jnp.transpose(trecv[:, 2].reshape(128, 128))

    def first_step(y, carry):
        solid = solid_p[y]
        for comp in range(19):
            s1[SLOT[comp], y + 1, 8:24, :] = blend(rel[comp, y], pv[OPPOSITE[comp], y], solid)
        return carry

    lax.fori_loop(0, 8, first_step, 0)
    for copy in early:
        copy.wait_recv()
    for side, comps, z, lane_z in ((0, ZP, 7, 15), (1, ZM, 24, 0)):
        solid = solid_z[:, lane_z, :]
        for n, comp in enumerate(comps):
            s1[SLOT[comp], 1:9, z, :] = blend(zab_in[side, 0, n], zab_in[side, 1, n], solid)
    for side, comps, y in ((0, YP, 0), (1, YM, 9)):
        solid = solid_h[64 * side + 16 : 64 * side + 32, :]
        for n, comp in enumerate(comps):
            s1[SLOT[comp], y, 8:24, :] = blend(yab_in[side, 0, n], yab_in[side, 1, n], solid)
    for n, (comp, dx, dy) in enumerate(EDGES):
        y, z = (0 if dy > 0 else 9), (7 if dx > 0 else 24)
        at = (0 if dy > 0 else 64) + (15 if dx > 0 else 32)
        s1[SLOT[comp], y, z : z + 1, :] = blend(cab_in[n, 0:1], cab_in[n, 1:2], solid_h[at : at + 1, :])

    pending = []

    def step(buf):
        def one(t, carry):
            y = lax.rem(t + 7, 8)
            g = [streamed(s1, comp, y) for comp in range(19)]
            solid = solid_p[y]
            for comp, value in enumerate(relax(g)):
                buf[SLOT[comp], y + 1, 8:24, :] = blend(value, g[OPPOSITE[comp]], solid)
            return carry

        sems = lambda n: (ls_sem.at[n], lr_sem.at[n])
        lax.fori_loop(0, 2, one, 0)
        copies = [
            remote(buf.at[0:5, 8, 8:24], buf.at[0:5, 0, 8:24], *sems(0), dev(0, 1)),
            remote(buf.at[5:10, 1, 8:24], buf.at[5:10, 9, 8:24], *sems(1), dev(0, -1)),
        ]
        for n, (comp, dx, dy) in enumerate(EDGES):
            y, z = (8 if dy > 0 else 1), (23 if dx > 0 else 8)
            csend[n, 0:1] = buf[SLOT[comp], y, z : z + 1, :]
            copies.append(remote(csend.at[n], crecv.at[n], *sems(2 + n), dev(dx, dy)))
        lax.fori_loop(2, 8, one, 0)
        for side, comps, z, dx in ((0, ZP, 23, 1), (1, ZM, 8, -1)):
            for n, comp in enumerate(comps):
                zsend[side, n] = buf[SLOT[comp], 1:9, z, :]
            copies.append(remote(zsend.at[side], zrecv.at[side], *sems(6 + side), dev(dx, 0)))
        for copy in copies:
            copy.wait_recv()
        pending.extend(copies)
        for side, comps, z in ((0, ZP, 7), (1, ZM, 24)):
            for n, comp in enumerate(comps):
                buf[SLOT[comp], 1:9, z, :] = zrecv[side, n]
        for n, (comp, dx, dy) in enumerate(EDGES):
            y, z = (0 if dy > 0 else 9), (7 if dx > 0 else 24)
            buf[SLOT[comp], y, z : z + 1, :] = crecv[n, 0:1]

    step(s2)
    for copy in early + moves + pending:
        copy.wait_send()


def finish(phase_next, solute_next, s2, phase_out, solute_out, out, buf, sems):
    copies = [
        pltpu.make_async_copy(phase_next, phase_out, sems.at[8]),
        pltpu.make_async_copy(solute_next, solute_out, sems.at[9]),
    ]
    for copy in copies:
        copy.start()
    for y in range(8):
        for comp in range(19):
            buf[comp, y] = streamed(s2, comp, y)
        copies.append(pltpu.make_async_copy(buf.at[:, y], out.at[:, y], sems.at[y]))
        copies[-1].start()
    for copy in copies:
        copy.wait()


def per_device(ngx, ngy, phase, solute, grain, grain_angle, inlet_flags, populations):
    vmem = pl.BlockSpec(memory_space=pltpu.VMEM)
    operands = (grain_angle, phase, solute, grain, inlet_flags, populations)
    hbm = pl.BlockSpec(memory_space=pltpu.HBM)
    phase_next, solute_next, s2 = pl.pallas_call(
        functools.partial(kernel, ngx, ngy),
        out_shape=[
            jax.ShapeDtypeStruct(phase.shape, jnp.float32),
            jax.ShapeDtypeStruct(solute.shape, jnp.float32),
            jax.ShapeDtypeStruct((19, 10, 32, 128), jnp.float32),
        ],
        in_specs=[hbm] * 6,
        out_specs=[vmem, vmem, vmem],
        scratch_shapes=[
            pltpu.SMEM((16,), jnp.float32),
            pltpu.VMEM((8, 8, 256), jnp.float32),
            pltpu.VMEM((8, 8, 256), jnp.float32),
            pltpu.VMEM((8, 8, 256), jnp.int32),
            pltpu.VMEM((8, 16), jnp.int32),
            pltpu.VMEM((19, 8, 16, 128), jnp.float32),
            pltpu.VMEM((19, 8, 16, 128), jnp.float32),
            pltpu.VMEM((2, 4, 8, 256), jnp.float32),
            pltpu.VMEM((2, 4, 8, 256), jnp.float32),
            pltpu.VMEM((2, 2, 8, 256), jnp.float32),
            pltpu.VMEM((4, 8, 128), jnp.float32),
            pltpu.VMEM((4, 8, 128), jnp.float32),
            pltpu.VMEM((ngx, 3, 8, 128), jnp.float32),
            pltpu.VMEM((ngx, 3, 8, 128), jnp.float32),
            pltpu.VMEM((8, 16, 128), jnp.float32),
            pltpu.VMEM((8, 16, 128), jnp.float32),
            pltpu.VMEM((8, 16, 128), jnp.float32),
            pltpu.VMEM((128, 128), jnp.float32),
            pltpu.VMEM((19, 10, 32, 128), jnp.float32),
            pltpu.VMEM((2, 2, 5, 16, 128), jnp.float32),
            pltpu.VMEM((2, 2, 5, 16, 128), jnp.float32),
            pltpu.VMEM((2, 2, 5, 8, 128), jnp.float32),
            pltpu.VMEM((2, 2, 5, 8, 128), jnp.float32),
            pltpu.VMEM((4, 8, 128), jnp.float32),
            pltpu.VMEM((4, 8, 128), jnp.float32),
            pltpu.VMEM((2, 5, 8, 128), jnp.float32),
            pltpu.VMEM((2, 5, 8, 128), jnp.float32),
            pltpu.VMEM((4, 8, 128), jnp.float32),
            pltpu.VMEM((4, 8, 128), jnp.float32),
            pltpu.SemaphoreType.DMA((6,)),
            pltpu.SemaphoreType.DMA((10,)),
            pltpu.SemaphoreType.DMA((10,)),
            pltpu.SemaphoreType.DMA((8,)),
            pltpu.SemaphoreType.DMA((8,)),
            pltpu.SemaphoreType.DMA((ngx - 1,)),
            pltpu.SemaphoreType.DMA((ngx - 1,)),
            pltpu.SemaphoreType.DMA((8,)),
            pltpu.SemaphoreType.DMA((8,)),
        ],
        compiler_params=pltpu.CompilerParams(
            collective_id=0, has_side_effects=True, vmem_limit_bytes=40 * 1024 * 1024
        ),
    )(*[pltpu.with_memory_space_constraint(a, pltpu.HBM) for a in operands])
    return pl.pallas_call(
        finish,
        out_shape=[
            jax.ShapeDtypeStruct(phase.shape, jnp.float32),
            jax.ShapeDtypeStruct(solute.shape, jnp.float32),
            jax.ShapeDtypeStruct(populations.shape, jnp.float32),
        ],
        in_specs=[vmem] * 3,
        out_specs=[hbm] * 3,
        scratch_shapes=[pltpu.VMEM((19, 8, 16, 128), jnp.float32), pltpu.SemaphoreType.DMA((10,))],
        compiler_params=pltpu.CompilerParams(vmem_limit_bytes=40 * 1024 * 1024),
    )(phase_next, solute_next, s2)


def solution(mesh):
    return jax.shard_map(
        functools.partial(per_device, mesh.shape["gx"], mesh.shape["gy"]),
        mesh=mesh,
        in_specs=(
            P("gx", "gy", None),
            P("gx", "gy", None),
            P("gx", "gy", None),
            P(),
            P("gy", "gx"),
            P(None, "gy", "gx", None),
        ),
        out_specs=(P("gx", "gy", None), P("gx", "gy", None), P(None, "gy", "gx", None)),
        check_vma=False,
    )
```

```python
import functools

import jax
import jax.numpy as jnp
from jax import lax
from jax.experimental import pallas as pl
from jax.experimental.pallas import tpu as pltpu
from jax.sharding import PartitionSpec as P

MESH = pl.DeviceIdType.MESH
VELOCITY = (
    (0, 0, 0),
    (1, 0, 0),
    (-1, 0, 0),
    (0, 1, 0),
    (0, -1, 0),
    (0, 0, 1),
    (0, 0, -1),
    (1, 1, 0),
    (-1, -1, 0),
    (1, -1, 0),
    (-1, 1, 0),
    (1, 0, 1),
    (-1, 0, -1),
    (1, 0, -1),
    (-1, 0, 1),
    (0, 1, 1),
    (0, -1, -1),
    (0, 1, -1),
    (0, -1, 1),
)
YP = (3, 7, 10, 15, 17)
YM = (4, 8, 9, 16, 18)
ZP = (5, 11, 14, 15, 18)
ZM = (6, 12, 13, 16, 17)
ORDER = YP + YM + (0, 1, 2, 5, 6, 11, 12, 13, 14)
SLOT = tuple(ORDER.index(comp) for comp in range(19))
EDGES = ((15, 1, 1), (16, -1, -1), (17, -1, 1), (18, 1, -1))
OPPOSITE = (0, 2, 1, 4, 3, 6, 5, 8, 7, 10, 9, 12, 11, 14, 13, 16, 15, 18, 17)
BODY_FORCE = 0.01
GRAINS = 16


def swap_groups(values, axis, size):
    values = list(values)
    length = values[0].shape[axis]
    group = lax.broadcasted_iota(jnp.int32, values[0].shape, axis) // size
    for bit in (1, 2, 4):
        upper = (group & bit) != 0
        for i in range(8):
            if i & bit == 0:
                low, high = values[i], values[i + bit]
                values[i] = jnp.where(upper, pltpu.roll(high, size * bit, axis), low)
                values[i + bit] = jnp.where(upper, high, pltpu.roll(low, length - size * bit, axis))
    return values


def relax(g):
    dif = {i: g[i] - g[i + 1] for i in range(1, 19, 2)}
    add = {i: g[i] + g[i + 1] for i in range(1, 19, 2)}
    axes = add[1] + add[3] + add[5]
    diag = (add[7] + add[9]) + (add[11] + add[13]) + (add[15] + add[17])
    dens = 12.0 * g[0] + 2.0 * axes + diag
    mom_x = 2.0 * dif[1] + ((dif[7] + dif[9]) + (dif[11] + dif[13]))
    mom_y = 2.0 * dif[3] + ((dif[7] - dif[9]) + (dif[15] + dif[17]))
    mom_z = 2.0 * dif[5] + ((dif[11] - dif[13]) + (dif[15] - dif[17]))
    inv = 1.0 / dens
    ux = (mom_x + 18.0 * BODY_FORCE) * inv
    uy = mom_y * inv
    uz = mom_z * inv
    scaled = dens * (1.25 / 36.0)
    base = scaled * (1.0 - 1.5 * (ux * ux + uy * uy + uz * uz))
    square = 4.5 * scaled
    linear = 3.0 * scaled
    along = {
        1: ux,
        3: uy,
        5: uz,
        7: ux + uy,
        9: ux - uy,
        11: ux + uz,
        13: ux - uz,
        15: uy + uz,
        17: uy - uz,
    }
    relaxed = [None] * 19
    relaxed[0] = base - 0.25 * g[0]
    for i, a in along.items():
        even = base + square * (a * a)
        odd = linear * a
        if VELOCITY[i][0]:
            odd = odd + 3.0 * BODY_FORCE
        relaxed[i] = even + odd - 0.25 * g[i]
        relaxed[i + 1] = even - odd - 0.25 * g[i + 1]
    return relaxed


def blend(relaxed, back, solid):
    return relaxed + solid * (back - relaxed)


def next_phase(ph, lap, dx, dy, so, cos_cell, sin_cell):
    gx, gy = 0.5 * dx, 0.5 * dy
    sx, sy = gx * gx, gy * gy
    denom = sx + sy + 0.25
    inv = 1.0 / (denom * denom)
    cos_four = (sx * sx - 6.0 * sx * sy + sy * sy) * inv
    sin_four = 4.0 * gx * gy * (sx - sy) * inv
    aniso = 1.0 + 0.3 * (cos_four * cos_cell + sin_four * sin_cell)
    bulk = 1.0 - ph * ph
    return ph + 0.08 * aniso * aniso * (lap + ph - ph * ph * ph - 1.5 * so * bulk * bulk)


def solid_of(ph):
    return jnp.clip(0.5 * (1.0 + ph), 0.0, 1.0)


def streamed(buf, comp, y):
    vx, vy, vz = VELOCITY[comp]
    value = buf[SLOT[comp], y + 1 - vy, 8 - vz : 24 - vz, :]
    if vx:
        value = pltpu.roll(value, vx % 128, 1)
    return value


def kernel(
    ngx, ngy,
    angle_in, phase_in, solute_in, grain_in, flags_in, pops,
    phase_out, solute_out, s2,
    angle, phase, solute, grain, flags, pv, rel, ysend, yrecv, xrecv, dsend, drecv,
    tsend, trecv, solid_p, closed, solid_z, solid_h, s1,
    yab, yab_in, zab, zab_in, cab, cab_in, zsend, zrecv, csend, crecv,
    in_sem, fs_sem, fr_sem, bs_sem, br_sem, ts_sem, tr_sem, ls_sem, lr_sem,
):
    me_x, me_y = lax.axis_index("gx"), lax.axis_index("gy")

    def dev(dx, dy):
        return {"gx": lax.rem(me_x + dx + ngx, ngx), "gy": lax.rem(me_y + dy + ngy, ngy)}

    def remote(src, dst, send, recv, device):
        copy = pltpu.make_async_remote_copy(
            src_ref=src, dst_ref=dst, send_sem=send, recv_sem=recv, device_id=device, device_id_type=MESH
        )
        copy.start()
        return copy

    far_first = sorted(range(1, ngx), key=lambda d: (abs(d % 8 - 4), abs(d - 8)))
    partners = [dev(dx, dy) for _, dx, dy in EDGES]
    partners += [dev(d, 0) for d in far_first] + [dev(0, 1), dev(0, -1)]
    barrier = pltpu.get_barrier_semaphore()
    for device in partners:
        pl.semaphore_signal(barrier, inc=1, device_id=device, device_id_type=MESH)
    loads = []
    for n, (src, dst) in enumerate(
        ((phase_in, phase), (solute_in, solute), (angle_in, angle), (grain_in, grain), (flags_in, flags), (pops, pv))
    ):
        loads.append(pltpu.make_async_copy(src, dst, in_sem.at[n]))
        loads[-1].start()
    loads[0].wait()
    loads[1].wait()
    loads[3].wait()
    for side, edge, second in ((0, 7, 6), (1, 0, 1)):
        ysend[side, 0] = phase[:, edge, :]
        ysend[side, 1] = phase[:, second, :]
        ysend[side, 2] = solute[:, edge, :]
        ysend[side, 3] = grain[:, edge, :].astype(jnp.float32)
    for n, (_, dx, dy) in enumerate(EDGES):
        line = phase[7 if dx > 0 else 0, 7 if dy > 0 else 0 : 8 if dy > 0 else 1, :]
        dsend[n, 0:1] = line[:, :128]
        dsend[n, 1:2] = line[:, 128:]
    pl.semaphore_wait(barrier, len(partners))

    faces = []
    for n, (_, dx, dy) in enumerate(EDGES):
        faces.append(remote(dsend.at[n], drecv.at[n], fs_sem.at[6 + n], fr_sem.at[6 + n], dev(dx, dy)))
    for side, step, layer in ((0, 1, 7), (1, -1, 0)):
        for field, ref in enumerate((phase, solute)):
            n = 2 + 2 * side + field
            faces.append(remote(ref.at[layer], xrecv.at[side, field], fs_sem.at[n], fr_sem.at[n], dev(step, 0)))
    for side, step in ((0, 1), (1, -1)):
        faces.append(remote(ysend.at[side], yrecv.at[side], fs_sem.at[side], fr_sem.at[side], dev(0, step)))

    loads[4].wait()
    open_row = jnp.concatenate([flags[y : y + 1, :] for y in range(8)], axis=1)
    first = lax.broadcasted_iota(jnp.int32, (128, 128), 0) == 0
    closed[...] = jnp.transpose(jnp.where(first & (open_row == 0), 1.0, 0.0)).reshape(8, 16, 128)

    loads[5].wait()

    def first_relax(t, carry):
        y = lax.rem(t + 7, 8)
        g = [pv[comp, y] for comp in range(19)]
        shut = closed[y] > 0.5
        for comp, value in enumerate(relax(g)):
            rel[comp, y] = jnp.where(shut, g[OPPOSITE[comp]], value)
        return carry

    lax.fori_loop(0, 2, first_relax, 0, unroll=2)
    early = []
    for side, comps, y in ((0, YP, 7), (1, YM, 0)):
        for n, comp in enumerate(comps):
            yab[side, 0, n] = rel[comp, y]
            yab[side, 1, n] = pv[OPPOSITE[comp], y]
    for copy in faces:
        copy.wait_send()
    for side, step in ((0, 1), (1, -1)):
        early.append(remote(yab.at[side], yab_in.at[side], bs_sem.at[2 + side], br_sem.at[2 + side], dev(0, step)))
    lax.fori_loop(2, 8, first_relax, 0, unroll=2)
    for side, comps, z, dx in ((0, ZP, 15, 1), (1, ZM, 0, -1)):
        for n, comp in enumerate(comps):
            zab[side, 0, n] = rel[comp, :, z, :]
            zab[side, 1, n] = pv[OPPOSITE[comp], :, z, :]
        early.append(remote(zab.at[side], zab_in.at[side], bs_sem.at[side], br_sem.at[side], dev(dx, 0)))
    for n, (comp, dx, dy) in enumerate(EDGES):
        y, z = (7 if dy > 0 else 0), (15 if dx > 0 else 0)
        cab[n, 0:1] = rel[comp, y, z : z + 1, :]
        cab[n, 1:2] = pv[OPPOSITE[comp], y, z : z + 1, :]
        early.append(remote(cab.at[n], cab_in.at[n], bs_sem.at[4 + n], br_sem.at[4 + n], dev(dx, dy)))

    loads[2].wait()
    lane = lax.broadcasted_iota(jnp.int32, (8, 128), 1)
    table = jnp.zeros((8, 128), jnp.float32)
    for which in range(GRAINS):
        table = jnp.where(lane == which, angle[which], table)
    cos_table, sin_table = jnp.cos(4.0 * table), jnp.sin(4.0 * table)
    cos_of = [jnp.broadcast_to(cos_table[:, i : i + 1], (8, 256)) for i in range(GRAINS)]
    sin_of = [jnp.broadcast_to(sin_table[:, i : i + 1], (8, 256)) for i in range(GRAINS)]

    def trig(ids):
        c, s = cos_of, sin_of
        for bit in (1, 2, 4, 8):
            on = (ids & bit) != 0
            c = [jnp.where(on, c[2 * i + 1], c[2 * i]) for i in range(len(c) // 2)]
            s = [jnp.where(on, s[2 * i + 1], s[2 * i]) for i in range(len(s) // 2)]
        return c[0], s[0]

    cells = [trig(grain[x]) for x in range(8)]
    for copy in faces:
        copy.wait_recv()
    row = lax.broadcasted_iota(jnp.int32, (8, 256), 0)

    def around(ref, field, x):
        value = ref[x]
        xplus = ref[x + 1] if x < 7 else xrecv[1, field]
        xminus = ref[x - 1] if x > 0 else xrecv[0, field]
        yplus = jnp.where(row == 7, yrecv[1, 2 * field, x : x + 1, :], pltpu.roll(value, 7, 0))
        yminus = jnp.where(row == 0, yrecv[0, 2 * field, x : x + 1, :], pltpu.roll(value, 1, 0))
        zplus, zminus = pltpu.roll(value, 255, 1), pltpu.roll(value, 1, 1)
        laplace = (xplus + xminus) + (yplus + yminus) + (zplus + zminus) - 6.0 * value
        return value, laplace, xplus - xminus, yplus - yminus

    solids = []
    for x in range(8):
        ph, lap, dx, dy = around(phase, 0, x)
        ph_next = next_phase(ph, lap, dx, dy, solute[x], *cells[x])
        phase_out[x] = ph_next
        solids.append(solid_of(ph_next))

    beyond = []
    for side in range(2):
        ph, second, so, ids = (yrecv[side, n] for n in range(4))
        inner = ysend[1 - side, 0]
        yplus, yminus = (inner, second) if side == 0 else (second, inner)
        lines = {}
        for n, (_, dx, dy) in enumerate(EDGES):
            if dy == (1 if side == 0 else -1):
                lines[dx] = jnp.concatenate([drecv[n, 0:1], drecv[n, 1:2]], axis=1)
        xplus = jnp.where(row == 7, lines[-1], pltpu.roll(ph, 7, 0))
        xminus = jnp.where(row == 0, lines[1], pltpu.roll(ph, 1, 0))
        lap = (xplus + xminus) + (yplus + yminus) + (pltpu.roll(ph, 255, 1) + pltpu.roll(ph, 1, 1)) - 6.0 * ph
        ph_next = next_phase(ph, lap, xplus - xminus, yplus - yminus, so, *trig(ids.astype(jnp.int32)))
        beyond.append(solid_of(ph_next))

    rows = swap_groups(solids, 0, 1)
    tiles = []
    for half in range(2):
        tiles += swap_groups([r[:, 128 * half : 128 * half + 128] for r in rows], 1, 16)
    last_lane = (lane & 15) == 15
    for k in range(ngx):
        tsend[k, 0] = tiles[k]
        tsend[k, 1] = jnp.where(last_lane, tiles[k - 1], tiles[(k + 1) % ngx])
        below = pltpu.roll(beyond[0], (272 - 16 * k) % 256, 1)[:, :128]
        above = pltpu.roll(beyond[1], (336 - 16 * k) % 256, 1)[:, :128]
        tsend[k, 2] = jnp.where(lane < 64, below, above)
    moves = []
    for d in far_first:
        device = dev(d, 0)
        moves.append(
            remote(tsend.at[device["gx"]], trecv.at[me_x], ts_sem.at[d - 1], tr_sem.at[d - 1], device)
        )
    trecv[me_x] = tsend[me_x]
    for x in range(8):
        so, lap_so, _, _ = around(solute, 1, x)
        solute_out[x] = so + 0.16 * lap_so + 0.5 * (phase_out[x] - phase[x])
    for copy in moves:
        copy.wait_recv()
    solid_p[...] = jnp.maximum(jnp.transpose(trecv[:, 0].reshape(128, 128)).reshape(8, 16, 128), closed[...])
    solid_z[...] = jnp.transpose(trecv[:, 1].reshape(128, 128)).reshape(8, 16, 128)
    solid_h[...] = jnp.transpose(trecv[:, 2].reshape(128, 128))

    def first_step(y, carry):
        solid = solid_p[y]
        for comp in range(19):
            s1[SLOT[comp], y + 1, 8:24, :] = blend(rel[comp, y], pv[OPPOSITE[comp], y], solid)
        return carry

    for y in (0, 1, 6, 7):
        first_step(y, 0)
    for copy in early:
        copy.wait_recv()
    for side, comps, z, lane_z in ((0, ZP, 7, 15), (1, ZM, 24, 0)):
        solid = solid_z[:, lane_z, :]
        for n, comp in enumerate(comps):
            s1[SLOT[comp], 1:9, z, :] = blend(zab_in[side, 0, n], zab_in[side, 1, n], solid)
    for side, comps, y in ((0, YP, 0), (1, YM, 9)):
        solid = solid_h[64 * side + 16 : 64 * side + 32, :]
        for n, comp in enumerate(comps):
            s1[SLOT[comp], y, 8:24, :] = blend(yab_in[side, 0, n], yab_in[side, 1, n], solid)
    for n, (comp, dx, dy) in enumerate(EDGES):
        y, z = (0 if dy > 0 else 9), (7 if dx > 0 else 24)
        at = (0 if dy > 0 else 64) + (15 if dx > 0 else 32)
        s1[SLOT[comp], y, z : z + 1, :] = blend(cab_in[n, 0:1], cab_in[n, 1:2], solid_h[at : at + 1, :])

    pending = []

    def step(buf):
        def one(t, carry):
            y = lax.rem(t + 7, 8)
            g = [streamed(s1, comp, y) for comp in range(19)]
            solid = solid_p[y]
            for comp, value in enumerate(relax(g)):
                buf[SLOT[comp], y + 1, 8:24, :] = blend(value, g[OPPOSITE[comp]], solid)
            return carry

        sems = lambda n: (ls_sem.at[n], lr_sem.at[n])
        lax.fori_loop(0, 2, one, 0, unroll=2)
        copies = []
        for n, (comp, dx, dy) in enumerate(EDGES):
            y, z = (8 if dy > 0 else 1), (23 if dx > 0 else 8)
            csend[n, 0:1] = buf[SLOT[comp], y, z : z + 1, :]
            copies.append(remote(csend.at[n], crecv.at[n], *sems(2 + n), dev(dx, dy)))
        copies += [
            remote(buf.at[0:5, 8, 8:24], buf.at[0:5, 0, 8:24], *sems(0), dev(0, 1)),
            remote(buf.at[5:10, 1, 8:24], buf.at[5:10, 9, 8:24], *sems(1), dev(0, -1)),
        ]
        lax.fori_loop(2, 6, first_step, 0, unroll=2)
        lax.fori_loop(2, 8, one, 0, unroll=2)
        for side, comps, z, dx in ((0, ZP, 23, 1), (1, ZM, 8, -1)):
            for n, comp in enumerate(comps):
                zsend[side, n] = buf[SLOT[comp], 1:9, z, :]
            copies.append(remote(zsend.at[side], zrecv.at[side], *sems(6 + side), dev(dx, 0)))
        for copy in copies:
            copy.wait_recv()
        pending.extend(copies)
        for side, comps, z in ((0, ZP, 7), (1, ZM, 24)):
            for n, comp in enumerate(comps):
                buf[SLOT[comp], 1:9, z, :] = zrecv[side, n]
        for n, (comp, dx, dy) in enumerate(EDGES):
            y, z = (0 if dy > 0 else 9), (7 if dx > 0 else 24)
            buf[SLOT[comp], y, z : z + 1, :] = crecv[n, 0:1]

    step(s2)
    for copy in early + moves + pending:
        copy.wait_send()


def finish(phase_next, solute_next, s2, phase_out, solute_out, out, buf, sems):
    copies = [
        pltpu.make_async_copy(phase_next, phase_out, sems.at[8]),
        pltpu.make_async_copy(solute_next, solute_out, sems.at[9]),
    ]
    for copy in copies:
        copy.start()
    for y in range(8):
        for comp in range(19):
            buf[comp, y] = streamed(s2, comp, y)
        copies.append(pltpu.make_async_copy(buf.at[:, y], out.at[:, y], sems.at[y]))
        copies[-1].start()
    for copy in copies:
        copy.wait()


def per_device(ngx, ngy, phase, solute, grain, grain_angle, inlet_flags, populations):
    vmem = pl.BlockSpec(memory_space=pltpu.VMEM)
    operands = (grain_angle, phase, solute, grain, inlet_flags, populations)
    hbm = pl.BlockSpec(memory_space=pltpu.HBM)
    phase_next, solute_next, s2 = pl.pallas_call(
        functools.partial(kernel, ngx, ngy),
        out_shape=[
            jax.ShapeDtypeStruct(phase.shape, jnp.float32),
            jax.ShapeDtypeStruct(solute.shape, jnp.float32),
            jax.ShapeDtypeStruct((19, 10, 32, 128), jnp.float32),
        ],
        in_specs=[hbm] * 6,
        out_specs=[vmem, vmem, vmem],
        scratch_shapes=[
            pltpu.SMEM((16,), jnp.float32),
            pltpu.VMEM((8, 8, 256), jnp.float32),
            pltpu.VMEM((8, 8, 256), jnp.float32),
            pltpu.VMEM((8, 8, 256), jnp.int32),
            pltpu.VMEM((8, 16), jnp.int32),
            pltpu.VMEM((19, 8, 16, 128), jnp.float32),
            pltpu.VMEM((19, 8, 16, 128), jnp.float32),
            pltpu.VMEM((2, 4, 8, 256), jnp.float32),
            pltpu.VMEM((2, 4, 8, 256), jnp.float32),
            pltpu.VMEM((2, 2, 8, 256), jnp.float32),
            pltpu.VMEM((4, 8, 128), jnp.float32),
            pltpu.VMEM((4, 8, 128), jnp.float32),
            pltpu.VMEM((ngx, 3, 8, 128), jnp.float32),
            pltpu.VMEM((ngx, 3, 8, 128), jnp.float32),
            pltpu.VMEM((8, 16, 128), jnp.float32),
            pltpu.VMEM((8, 16, 128), jnp.float32),
            pltpu.VMEM((8, 16, 128), jnp.float32),
            pltpu.VMEM((128, 128), jnp.float32),
            pltpu.VMEM((19, 10, 32, 128), jnp.float32),
            pltpu.VMEM((2, 2, 5, 16, 128), jnp.float32),
            pltpu.VMEM((2, 2, 5, 16, 128), jnp.float32),
            pltpu.VMEM((2, 2, 5, 8, 128), jnp.float32),
            pltpu.VMEM((2, 2, 5, 8, 128), jnp.float32),
            pltpu.VMEM((4, 8, 128), jnp.float32),
            pltpu.VMEM((4, 8, 128), jnp.float32),
            pltpu.VMEM((2, 5, 8, 128), jnp.float32),
            pltpu.VMEM((2, 5, 8, 128), jnp.float32),
            pltpu.VMEM((4, 8, 128), jnp.float32),
            pltpu.VMEM((4, 8, 128), jnp.float32),
            pltpu.SemaphoreType.DMA((6,)),
            pltpu.SemaphoreType.DMA((10,)),
            pltpu.SemaphoreType.DMA((10,)),
            pltpu.SemaphoreType.DMA((8,)),
            pltpu.SemaphoreType.DMA((8,)),
            pltpu.SemaphoreType.DMA((ngx - 1,)),
            pltpu.SemaphoreType.DMA((ngx - 1,)),
            pltpu.SemaphoreType.DMA((8,)),
            pltpu.SemaphoreType.DMA((8,)),
        ],
        compiler_params=pltpu.CompilerParams(
            collective_id=0, has_side_effects=True, vmem_limit_bytes=40 * 1024 * 1024
        ),
    )(*[pltpu.with_memory_space_constraint(a, pltpu.HBM) for a in operands])
    return pl.pallas_call(
        finish,
        out_shape=[
            jax.ShapeDtypeStruct(phase.shape, jnp.float32),
            jax.ShapeDtypeStruct(solute.shape, jnp.float32),
            jax.ShapeDtypeStruct(populations.shape, jnp.float32),
        ],
        in_specs=[vmem] * 3,
        out_specs=[hbm] * 3,
        scratch_shapes=[pltpu.VMEM((19, 8, 16, 128), jnp.float32), pltpu.SemaphoreType.DMA((10,))],
        compiler_params=pltpu.CompilerParams(vmem_limit_bytes=40 * 1024 * 1024),
    )(phase_next, solute_next, s2)


def solution(mesh):
    return jax.shard_map(
        functools.partial(per_device, mesh.shape["gx"], mesh.shape["gy"]),
        mesh=mesh,
        in_specs=(
            P("gx", "gy", None),
            P("gx", "gy", None),
            P("gx", "gy", None),
            P(),
            P("gy", "gx"),
            P(None, "gy", "gx", None),
        ),
        out_specs=(P("gx", "gy", None), P("gx", "gy", None), P(None, "gy", "gx", None)),
        check_vma=False,
    )
```

```python
import functools

import jax
import jax.numpy as jnp
from jax import lax
from jax.experimental import pallas as pl
from jax.experimental.pallas import tpu as pltpu
from jax.sharding import PartitionSpec as P

MESH = pl.DeviceIdType.MESH
VELOCITY = (
    (0, 0, 0),
    (1, 0, 0),
    (-1, 0, 0),
    (0, 1, 0),
    (0, -1, 0),
    (0, 0, 1),
    (0, 0, -1),
    (1, 1, 0),
    (-1, -1, 0),
    (1, -1, 0),
    (-1, 1, 0),
    (1, 0, 1),
    (-1, 0, -1),
    (1, 0, -1),
    (-1, 0, 1),
    (0, 1, 1),
    (0, -1, -1),
    (0, 1, -1),
    (0, -1, 1),
)
YP = (3, 7, 10, 15, 17)
YM = (4, 8, 9, 16, 18)
ZP = (5, 11, 14, 15, 18)
ZM = (6, 12, 13, 16, 17)
ORDER = YP + YM + (0, 1, 2, 5, 6, 11, 12, 13, 14)
SLOT = tuple(ORDER.index(comp) for comp in range(19))
EDGES = ((15, 1, 1), (16, -1, -1), (17, -1, 1), (18, 1, -1))
OPPOSITE = (0, 2, 1, 4, 3, 6, 5, 8, 7, 10, 9, 12, 11, 14, 13, 16, 15, 18, 17)
BODY_FORCE = 0.01
GRAINS = 16


def swap_groups(values, axis, size):
    values = list(values)
    length = values[0].shape[axis]
    group = lax.broadcasted_iota(jnp.int32, values[0].shape, axis) // size
    for bit in (1, 2, 4):
        upper = (group & bit) != 0
        for i in range(8):
            if i & bit == 0:
                low, high = values[i], values[i + bit]
                values[i] = jnp.where(upper, pltpu.roll(high, size * bit, axis), low)
                values[i + bit] = jnp.where(upper, high, pltpu.roll(low, length - size * bit, axis))
    return values


def relax(g):
    dif = {i: g[i] - g[i + 1] for i in range(1, 19, 2)}
    add = {i: g[i] + g[i + 1] for i in range(1, 19, 2)}
    axes = add[1] + add[3] + add[5]
    diag = (add[7] + add[9]) + (add[11] + add[13]) + (add[15] + add[17])
    dens = 12.0 * g[0] + 2.0 * axes + diag
    mom_x = 2.0 * dif[1] + ((dif[7] + dif[9]) + (dif[11] + dif[13]))
    mom_y = 2.0 * dif[3] + ((dif[7] - dif[9]) + (dif[15] + dif[17]))
    mom_z = 2.0 * dif[5] + ((dif[11] - dif[13]) + (dif[15] - dif[17]))
    inv = 1.0 / dens
    ux = (mom_x + 18.0 * BODY_FORCE) * inv
    uy = mom_y * inv
    uz = mom_z * inv
    scaled = dens * (1.25 / 36.0)
    base = scaled * (1.0 - 1.5 * (ux * ux + uy * uy + uz * uz))
    square = 4.5 * scaled
    linear = 3.0 * scaled
    along = {
        1: ux,
        3: uy,
        5: uz,
        7: ux + uy,
        9: ux - uy,
        11: ux + uz,
        13: ux - uz,
        15: uy + uz,
        17: uy - uz,
    }
    relaxed = [None] * 19
    relaxed[0] = base - 0.25 * g[0]
    for i, a in along.items():
        even = base + square * (a * a)
        odd = linear * a
        if VELOCITY[i][0]:
            odd = odd + 3.0 * BODY_FORCE
        relaxed[i] = even + odd - 0.25 * g[i]
        relaxed[i + 1] = even - odd - 0.25 * g[i + 1]
    return relaxed


def blend(relaxed, back, solid):
    return relaxed + solid * (back - relaxed)


def next_phase(ph, lap, dx, dy, so, cos_cell, sin_cell):
    gx, gy = 0.5 * dx, 0.5 * dy
    sx, sy = gx * gx, gy * gy
    denom = sx + sy + 0.25
    inv = 1.0 / (denom * denom)
    cos_four = (sx * sx - 6.0 * sx * sy + sy * sy) * inv
    sin_four = 4.0 * gx * gy * (sx - sy) * inv
    aniso = 1.0 + 0.3 * (cos_four * cos_cell + sin_four * sin_cell)
    bulk = 1.0 - ph * ph
    return ph + 0.08 * aniso * aniso * (lap + ph - ph * ph * ph - 1.5 * so * bulk * bulk)


def solid_of(ph):
    return jnp.clip(0.5 * (1.0 + ph), 0.0, 1.0)


def streamed(buf, comp, y):
    vx, vy, vz = VELOCITY[comp]
    value = buf[SLOT[comp], y + 1 - vy, 8 - vz : 24 - vz, :]
    if vx:
        value = pltpu.roll(value, vx % 128, 1)
    return value


def kernel(
    ngx, ngy,
    angle_in, phase_in, solute_in, grain_in, flags_in, pops,
    phase_out, solute_out, out,
    angle, phase, solute, grain, flags, pv, rel, ysend, yrecv, xrecv, dsend, drecv,
    tsend, trecv, solid_p, closed, solid_z, solid_h, s1, s2,
    yab, yab_in, zab, zab_in, cab, cab_in, zsend, zrecv, csend, crecv,
    in_sem, fs_sem, fr_sem, bs_sem, br_sem, ts_sem, tr_sem, ls_sem, lr_sem,
):
    me_x, me_y = lax.axis_index("gx"), lax.axis_index("gy")

    def dev(dx, dy):
        return {"gx": lax.rem(me_x + dx + ngx, ngx), "gy": lax.rem(me_y + dy + ngy, ngy)}

    def remote(src, dst, send, recv, device):
        copy = pltpu.make_async_remote_copy(
            src_ref=src, dst_ref=dst, send_sem=send, recv_sem=recv, device_id=device, device_id_type=MESH
        )
        copy.start()
        return copy

    far_first = sorted(range(1, ngx), key=lambda d: (abs(d % 8 - 4), abs(d - 8)))
    partners = [dev(dx, dy) for _, dx, dy in EDGES]
    partners += [dev(d, 0) for d in far_first] + [dev(0, 1), dev(0, -1)]
    barrier = pltpu.get_barrier_semaphore()
    for device in partners:
        pl.semaphore_signal(barrier, inc=1, device_id=device, device_id_type=MESH)
    loads = []
    for n, (src, dst) in enumerate(
        ((phase_in, phase), (solute_in, solute), (angle_in, angle), (grain_in, grain), (flags_in, flags), (pops, pv))
    ):
        loads.append(pltpu.make_async_copy(src, dst, in_sem.at[n]))
        loads[-1].start()
    loads[0].wait()
    loads[1].wait()
    loads[3].wait()
    for side, edge, second in ((0, 7, 6), (1, 0, 1)):
        ysend[side, 0] = phase[:, edge, :]
        ysend[side, 1] = phase[:, second, :]
        ysend[side, 2] = solute[:, edge, :]
        ysend[side, 3] = grain[:, edge, :].astype(jnp.float32)
    for n, (_, dx, dy) in enumerate(EDGES):
        line = phase[7 if dx > 0 else 0, 7 if dy > 0 else 0 : 8 if dy > 0 else 1, :]
        dsend[n, 0:1] = line[:, :128]
        dsend[n, 1:2] = line[:, 128:]
    pl.semaphore_wait(barrier, len(partners))

    faces = []
    for n, (_, dx, dy) in enumerate(EDGES):
        faces.append(remote(dsend.at[n], drecv.at[n], fs_sem.at[6 + n], fr_sem.at[6 + n], dev(dx, dy)))
    for side, step, layer in ((0, 1, 7), (1, -1, 0)):
        for field, ref in enumerate((phase, solute)):
            n = 2 + 2 * side + field
            faces.append(remote(ref.at[layer], xrecv.at[side, field], fs_sem.at[n], fr_sem.at[n], dev(step, 0)))
    for side, step in ((0, 1), (1, -1)):
        faces.append(remote(ysend.at[side], yrecv.at[side], fs_sem.at[side], fr_sem.at[side], dev(0, step)))

    loads[4].wait()
    open_row = jnp.concatenate([flags[y : y + 1, :] for y in range(8)], axis=1)
    first = lax.broadcasted_iota(jnp.int32, (128, 128), 0) == 0
    closed[...] = jnp.transpose(jnp.where(first & (open_row == 0), 1.0, 0.0)).reshape(8, 16, 128)

    loads[5].wait()

    def first_relax(t, carry):
        y = lax.rem(t + 7, 8)
        g = [pv[comp, y] for comp in range(19)]
        shut = closed[y] > 0.5
        for comp, value in enumerate(relax(g)):
            rel[comp, y] = jnp.where(shut, g[OPPOSITE[comp]], value)
        return carry

    lax.fori_loop(0, 2, first_relax, 0, unroll=2)
    early = []
    for side, comps, y in ((0, YP, 7), (1, YM, 0)):
        for n, comp in enumerate(comps):
            yab[side, 0, n] = rel[comp, y]
            yab[side, 1, n] = pv[OPPOSITE[comp], y]
    for copy in faces[8:]:
        copy.wait_send()
    for side, step in ((0, 1), (1, -1)):
        early.append(remote(yab.at[side], yab_in.at[side], bs_sem.at[2 + side], br_sem.at[2 + side], dev(0, step)))
    lax.fori_loop(2, 8, first_relax, 0, unroll=2)
    for side, comps, z, dx in ((0, ZP, 15, 1), (1, ZM, 0, -1)):
        for n, comp in enumerate(comps):
            zab[side, 0, n] = rel[comp, :, z, :]
            zab[side, 1, n] = pv[OPPOSITE[comp], :, z, :]
        early.append(remote(zab.at[side], zab_in.at[side], bs_sem.at[side], br_sem.at[side], dev(dx, 0)))
    for n, (comp, dx, dy) in enumerate(EDGES):
        y, z = (7 if dy > 0 else 0), (15 if dx > 0 else 0)
        cab[n, 0:1] = rel[comp, y, z : z + 1, :]
        cab[n, 1:2] = pv[OPPOSITE[comp], y, z : z + 1, :]
        early.append(remote(cab.at[n], cab_in.at[n], bs_sem.at[4 + n], br_sem.at[4 + n], dev(dx, dy)))

    loads[2].wait()
    lane = lax.broadcasted_iota(jnp.int32, (8, 128), 1)
    table = jnp.zeros((8, 128), jnp.float32)
    for which in range(GRAINS):
        table = jnp.where(lane == which, angle[which], table)
    cos_table, sin_table = jnp.cos(4.0 * table), jnp.sin(4.0 * table)
    cos_of = [jnp.broadcast_to(cos_table[:, i : i + 1], (8, 256)) for i in range(GRAINS)]
    sin_of = [jnp.broadcast_to(sin_table[:, i : i + 1], (8, 256)) for i in range(GRAINS)]

    def trig(ids):
        c, s = cos_of, sin_of
        for bit in (1, 2, 4, 8):
            on = (ids & bit) != 0
            c = [jnp.where(on, c[2 * i + 1], c[2 * i]) for i in range(len(c) // 2)]
            s = [jnp.where(on, s[2 * i + 1], s[2 * i]) for i in range(len(s) // 2)]
        return c[0], s[0]

    cells = [trig(grain[x]) for x in range(8)]
    for copy in faces:
        copy.wait_recv()
    row = lax.broadcasted_iota(jnp.int32, (8, 256), 0)

    def around(ref, field, x):
        value = ref[x]
        xplus = ref[x + 1] if x < 7 else xrecv[1, field]
        xminus = ref[x - 1] if x > 0 else xrecv[0, field]
        yplus = jnp.where(row == 7, yrecv[1, 2 * field, x : x + 1, :], pltpu.roll(value, 7, 0))
        yminus = jnp.where(row == 0, yrecv[0, 2 * field, x : x + 1, :], pltpu.roll(value, 1, 0))
        zplus, zminus = pltpu.roll(value, 255, 1), pltpu.roll(value, 1, 1)
        laplace = (xplus + xminus) + (yplus + yminus) + (zplus + zminus) - 6.0 * value
        return value, laplace, xplus - xminus, yplus - yminus

    solids = []
    for x in range(8):
        ph, lap, dx, dy = around(phase, 0, x)
        ph_next = next_phase(ph, lap, dx, dy, solute[x], *cells[x])
        phase_out[x] = ph_next
        solids.append(solid_of(ph_next))

    beyond = []
    for side in range(2):
        ph, second, so, ids = (yrecv[side, n] for n in range(4))
        inner = ysend[1 - side, 0]
        yplus, yminus = (inner, second) if side == 0 else (second, inner)
        lines = {}
        for n, (_, dx, dy) in enumerate(EDGES):
            if dy == (1 if side == 0 else -1):
                lines[dx] = jnp.concatenate([drecv[n, 0:1], drecv[n, 1:2]], axis=1)
        xplus = jnp.where(row == 7, lines[-1], pltpu.roll(ph, 7, 0))
        xminus = jnp.where(row == 0, lines[1], pltpu.roll(ph, 1, 0))
        lap = (xplus + xminus) + (yplus + yminus) + (pltpu.roll(ph, 255, 1) + pltpu.roll(ph, 1, 1)) - 6.0 * ph
        ph_next = next_phase(ph, lap, xplus - xminus, yplus - yminus, so, *trig(ids.astype(jnp.int32)))
        beyond.append(solid_of(ph_next))

    rows = swap_groups(solids, 0, 1)
    tiles = []
    for half in range(2):
        tiles += swap_groups([r[:, 128 * half : 128 * half + 128] for r in rows], 1, 16)
    last_lane = (lane & 15) == 15
    for k in range(ngx):
        tsend[k, 0] = tiles[k]
        tsend[k, 1] = jnp.where(last_lane, tiles[k - 1], tiles[(k + 1) % ngx])
        below = pltpu.roll(beyond[0], (272 - 16 * k) % 256, 1)[:, :128]
        above = pltpu.roll(beyond[1], (336 - 16 * k) % 256, 1)[:, :128]
        tsend[k, 2] = jnp.where(lane < 64, below, above)
    moves = []
    for d in far_first:
        device = dev(d, 0)
        moves.append(
            remote(tsend.at[device["gx"]], trecv.at[me_x], ts_sem.at[d - 1], tr_sem.at[d - 1], device)
        )
    trecv[me_x] = tsend[me_x]
    for x in range(8):
        so, lap_so, _, _ = around(solute, 1, x)
        solute_out[x] = so + 0.16 * lap_so + 0.5 * (phase_out[x] - phase[x])
    for copy in moves:
        copy.wait_recv()
    solid_p[...] = jnp.maximum(jnp.transpose(trecv[:, 0].reshape(128, 128)).reshape(8, 16, 128), closed[...])
    solid_z[...] = jnp.transpose(trecv[:, 1].reshape(128, 128)).reshape(8, 16, 128)
    solid_h[...] = jnp.transpose(trecv[:, 2].reshape(128, 128))

    def first_step(y, carry):
        solid = solid_p[y]
        for comp in range(19):
            s1[SLOT[comp], y + 1, 8:24, :] = blend(rel[comp, y], pv[OPPOSITE[comp], y], solid)
        return carry

    for y in (0, 1, 6, 7):
        first_step(y, 0)
    for copy in early:
        copy.wait_recv()
    for side, comps, z, lane_z in ((0, ZP, 7, 15), (1, ZM, 24, 0)):
        solid = solid_z[:, lane_z, :]
        for n, comp in enumerate(comps):
            s1[SLOT[comp], 1:9, z, :] = blend(zab_in[side, 0, n], zab_in[side, 1, n], solid)
    for side, comps, y in ((0, YP, 0), (1, YM, 9)):
        solid = solid_h[64 * side + 16 : 64 * side + 32, :]
        for n, comp in enumerate(comps):
            s1[SLOT[comp], y, 8:24, :] = blend(yab_in[side, 0, n], yab_in[side, 1, n], solid)
    for n, (comp, dx, dy) in enumerate(EDGES):
        y, z = (0 if dy > 0 else 9), (7 if dx > 0 else 24)
        at = (0 if dy > 0 else 64) + (15 if dx > 0 else 32)
        s1[SLOT[comp], y, z : z + 1, :] = blend(cab_in[n, 0:1], cab_in[n, 1:2], solid_h[at : at + 1, :])

    pending = []

    def step(buf):
        def one(t, carry):
            y = lax.rem(t + 7, 8)
            g = [streamed(s1, comp, y) for comp in range(19)]
            solid = solid_p[y]
            for comp, value in enumerate(relax(g)):
                buf[SLOT[comp], y + 1, 8:24, :] = blend(value, g[OPPOSITE[comp]], solid)
            return carry

        sems = lambda n: (ls_sem.at[n], lr_sem.at[n])
        lax.fori_loop(0, 2, one, 0, unroll=2)
        copies = []
        for n, (comp, dx, dy) in enumerate(EDGES):
            y, z = (8 if dy > 0 else 1), (23 if dx > 0 else 8)
            csend[n, 0:1] = buf[SLOT[comp], y, z : z + 1, :]
            copies.append(remote(csend.at[n], crecv.at[n], *sems(2 + n), dev(dx, dy)))
        copies += [
            remote(buf.at[0:5, 8, 8:24], buf.at[0:5, 0, 8:24], *sems(0), dev(0, 1)),
            remote(buf.at[5:10, 1, 8:24], buf.at[5:10, 9, 8:24], *sems(1), dev(0, -1)),
        ]
        lax.fori_loop(2, 6, first_step, 0, unroll=2)
        lax.fori_loop(2, 8, one, 0, unroll=2)
        for side, comps, z, dx in ((0, ZP, 23, 1), (1, ZM, 8, -1)):
            for n, comp in enumerate(comps):
                zsend[side, n] = buf[SLOT[comp], 1:9, z, :]
            copies.append(remote(zsend.at[side], zrecv.at[side], *sems(6 + side), dev(dx, 0)))
        def inner(y, carry):
            for comp in range(19):
                out[comp, y] = streamed(buf, comp, y)
            return carry

        lax.fori_loop(1, 7, inner, 0, unroll=2)
        for comp in range(19):
            if VELOCITY[comp][1] <= 0:
                out[comp, 0] = streamed(buf, comp, 0)
            if VELOCITY[comp][1] >= 0:
                out[comp, 7] = streamed(buf, comp, 7)
        for copy in copies:
            copy.wait_recv()
        pending.extend(copies)
        for side, comps, z in ((0, ZP, 0), (1, ZM, 15)):
            for n, comp in enumerate(comps):
                vx, vy, _ = VELOCITY[comp]
                value = zrecv[side, n]
                if vx:
                    value = pltpu.roll(value, vx % 128, 1)
                out[comp, max(vy, 0) : 8 + min(vy, 0), z, :] = value[max(-vy, 0) : 8 - max(vy, 0)]
        for n, (comp, dx, dy) in enumerate(EDGES):
            y, z = (0 if dy > 0 else 9), (7 if dx > 0 else 24)
            buf[SLOT[comp], y, z : z + 1, :] = crecv[n, 0:1]
        for comps, y in ((YP, 0), (YM, 7)):
            for comp in comps:
                out[comp, y] = streamed(buf, comp, y)

    step(s2)
    for copy in faces[:8] + early + moves + pending:
        copy.wait_send()


def finish(*refs):
    sems = refs[-1]
    phase_next, solute_next, pops_next, phase_out, solute_out, out = refs[:-1]
    pairs = [(phase_next, phase_out), (solute_next, solute_out)]
    pairs += [(pops_next.at[c : c + 5], out.at[c : c + 5]) for c in (0, 5, 10)]
    pairs += [(pops_next.at[15:19], out.at[15:19])]
    copies = [pltpu.make_async_copy(src, dst, sems.at[n]) for n, (src, dst) in enumerate(pairs)]
    for copy in copies:
        copy.start()
    for copy in copies:
        copy.wait()


def per_device(ngx, ngy, phase, solute, grain, grain_angle, inlet_flags, populations):
    vmem = pl.BlockSpec(memory_space=pltpu.VMEM)
    operands = (grain_angle, phase, solute, grain, inlet_flags, populations)
    hbm = pl.BlockSpec(memory_space=pltpu.HBM)
    phase_next, solute_next, pops_next = pl.pallas_call(
        functools.partial(kernel, ngx, ngy),
        out_shape=[
            jax.ShapeDtypeStruct(phase.shape, jnp.float32),
            jax.ShapeDtypeStruct(solute.shape, jnp.float32),
            jax.ShapeDtypeStruct(populations.shape, jnp.float32),
        ],
        in_specs=[hbm] * 6,
        out_specs=[vmem, vmem, vmem],
        scratch_shapes=[
            pltpu.SMEM((16,), jnp.float32),
            pltpu.VMEM((8, 8, 256), jnp.float32),
            pltpu.VMEM((8, 8, 256), jnp.float32),
            pltpu.VMEM((8, 8, 256), jnp.int32),
            pltpu.VMEM((8, 16), jnp.int32),
            pltpu.VMEM((19, 8, 16, 128), jnp.float32),
            pltpu.VMEM((19, 8, 16, 128), jnp.float32),
            pltpu.VMEM((2, 4, 8, 256), jnp.float32),
            pltpu.VMEM((2, 4, 8, 256), jnp.float32),
            pltpu.VMEM((2, 2, 8, 256), jnp.float32),
            pltpu.VMEM((4, 8, 128), jnp.float32),
            pltpu.VMEM((4, 8, 128), jnp.float32),
            pltpu.VMEM((ngx, 3, 8, 128), jnp.float32),
            pltpu.VMEM((ngx, 3, 8, 128), jnp.float32),
            pltpu.VMEM((8, 16, 128), jnp.float32),
            pltpu.VMEM((8, 16, 128), jnp.float32),
            pltpu.VMEM((8, 16, 128), jnp.float32),
            pltpu.VMEM((128, 128), jnp.float32),
            pltpu.VMEM((19, 10, 32, 128), jnp.float32),
            pltpu.VMEM((19, 10, 32, 128), jnp.float32),
            pltpu.VMEM((2, 2, 5, 16, 128), jnp.float32),
            pltpu.VMEM((2, 2, 5, 16, 128), jnp.float32),
            pltpu.VMEM((2, 2, 5, 8, 128), jnp.float32),
            pltpu.VMEM((2, 2, 5, 8, 128), jnp.float32),
            pltpu.VMEM((4, 8, 128), jnp.float32),
            pltpu.VMEM((4, 8, 128), jnp.float32),
            pltpu.VMEM((2, 5, 8, 128), jnp.float32),
            pltpu.VMEM((2, 5, 8, 128), jnp.float32),
            pltpu.VMEM((4, 8, 128), jnp.float32),
            pltpu.VMEM((4, 8, 128), jnp.float32),
            pltpu.SemaphoreType.DMA((6,)),
            pltpu.SemaphoreType.DMA((10,)),
            pltpu.SemaphoreType.DMA((10,)),
            pltpu.SemaphoreType.DMA((8,)),
            pltpu.SemaphoreType.DMA((8,)),
            pltpu.SemaphoreType.DMA((ngx - 1,)),
            pltpu.SemaphoreType.DMA((ngx - 1,)),
            pltpu.SemaphoreType.DMA((8,)),
            pltpu.SemaphoreType.DMA((8,)),
        ],
        compiler_params=pltpu.CompilerParams(
            collective_id=0, has_side_effects=True, vmem_limit_bytes=40 * 1024 * 1024
        ),
    )(*[pltpu.with_memory_space_constraint(a, pltpu.HBM) for a in operands])
    return pl.pallas_call(
        finish,
        out_shape=[
            jax.ShapeDtypeStruct(phase.shape, jnp.float32),
            jax.ShapeDtypeStruct(solute.shape, jnp.float32),
            jax.ShapeDtypeStruct(populations.shape, jnp.float32),
        ],
        in_specs=[vmem] * 3,
        out_specs=[hbm] * 3,
        scratch_shapes=[pltpu.SemaphoreType.DMA((6,))],
        compiler_params=pltpu.CompilerParams(vmem_limit_bytes=40 * 1024 * 1024),
    )(phase_next, solute_next, pops_next)


def solution(mesh):
    return jax.shard_map(
        functools.partial(per_device, mesh.shape["gx"], mesh.shape["gy"]),
        mesh=mesh,
        in_specs=(
            P("gx", "gy", None),
            P("gx", "gy", None),
            P("gx", "gy", None),
            P(),
            P("gy", "gx"),
            P(None, "gy", "gx", None),
        ),
        out_specs=(P("gx", "gy", None), P("gx", "gy", None), P(None, "gy", "gx", None)),
        check_vma=False,
    )
```
